32 devices in a mesh: lat: 8 (over z, core), vec: 4 (over y, x).
Axes of the slice: x: 2, y: 2, z: 4, core: 2. Of those that a mesh axis runs over, the one named last changes fastest.
Arguments:
- vectors: bfloat16 [4, 64, 128, 1024], P(None, 'vec', 'lat'), may hold values from -6 to 6
- classical_spins: float32 [3, 128, 1024], P(None, 'lat'), may hold values from -1 to 1, as said below
- coefficients: float32 [5], replicated, may hold values from 0.4 to 1.6
Outputs:
- rotated_spins: float32 [3, 128, 1024], P(None, 'lat')
- local_fields: float32 [3, 128, 1024], P(None, 'lat')
The draws below stay inside these ranges and needn't reach their ends.
Inputs may be any that keep to these rules, and one draw needn't show every extreme that they name: `classical_spins`: each site's spin has unit length.
All inputs are finite; a program needn't handle non-finite values.
Results may differ from the reference program's by a relative error of at most 0.0003.
Values sent between devices are 32-bit elements; how exact they have to be, the bound alone decides.
No kernel may reach another device: no remote copies, remote signals or barrier semaphores. Data moves between devices by JAX's collectives and lax.ppermute only.
A program may use at most 64 MiB of HBM per device.

```python
import jax
import jax.numpy as jnp
from jax import lax

NY = 1024
R_DEV = 16
STEPS = 4
NX = 128
VECTORS = 64
N_VEC = 4


def draw_classical_spins(key, part):
    raw = jax.random.normal(key, (3, NX, NY), jnp.float32)
    length = jnp.sqrt(jnp.sum(raw * raw, axis=0, keepdims=True))
    return raw / jnp.maximum(length, 0.001)


def shard_levels(rng, extent, shards, smallest, largest):
    factor_of = 1.0
    for axis_at, shards_of in shards:
        heights = jax.random.uniform(jax.random.fold_in(jax.random.fold_in(rng, 6), axis_at), (shards_of,), jnp.float32, smallest / len(shards), largest / len(shards))
        factor_of = factor_of * jnp.repeat(jnp.exp(heights), extent[axis_at] // shards_of).reshape((-1,) + (1,) * (len(extent) - 1 - axis_at))
    return factor_of


def gaussian(stream_key, extent, deviation, reach, pieces=(), dtype=jnp.bfloat16):
    level = shard_levels(stream_key, extent, pieces, -0.22, 0.18) if pieces else 1.0
    values = jax.random.normal(stream_key, extent, jnp.float32) * deviation * level
    return jnp.minimum(jnp.maximum(values, -reach), reach).astype(dtype)


def setup_inputs(seed: int = 0) -> dict:
    keys = jax.random.split(jax.random.key(seed), 4)
    return {
        "vectors": gaussian(keys[0], (4, VECTORS, NX, NY), 0.7071, 6.0, ((1, 4), (2, 8))),
        "classical_spins": draw_classical_spins(jax.random.fold_in(keys[3], 71), 0),
        "coefficients": jnp.clip(jax.random.uniform(keys[2], (STEPS + 1,), jnp.float32, 0.4, 1.6), 0.4, 1.6),
    }


coupling = 2.0
hopping = 1.0
inverse_bound = 1.0 / 6.5
time_step = 1.0

def exchange_term(states, spins_here):
    spin_x = spins_here[0][None]
    spin_y = spins_here[1][None]
    spin_z = spins_here[2][None]
    up_real, up_imag, down_real, down_imag = (states[0], states[1], states[2], states[3])
    return jnp.stack([spin_z * up_real + spin_x * down_real + spin_y * down_imag, spin_z * up_imag + spin_x * down_imag - spin_y * down_real, spin_x * up_real - spin_y * up_imag - spin_z * down_real, spin_x * up_imag + spin_y * up_real - spin_z * down_imag])

def spin_density(probes, weighted):
    along_x = lax.optimization_barrier(jnp.sum(probes[0] * weighted[2] + probes[1] * weighted[3] + probes[2] * weighted[0] + probes[3] * weighted[1], axis=0))
    along_y = lax.optimization_barrier(jnp.sum(probes[0] * weighted[3] - probes[1] * weighted[2] - probes[2] * weighted[1] + probes[3] * weighted[0], axis=0))
    along_z = lax.optimization_barrier(jnp.sum(probes[0] * weighted[0] + probes[1] * weighted[1] - probes[2] * weighted[2] - probes[3] * weighted[3], axis=0))
    return jnp.stack([along_x, along_y, along_z])

def rotate_spins(spins_now, fields):
    magnitude = jnp.sqrt(lax.optimization_barrier(jnp.sum(fields * fields, axis=0)))
    rotation_angle = time_step * magnitude
    cosine = jnp.cos(rotation_angle)
    sine_ratio = jnp.sinc(rotation_angle / jnp.pi)
    half_ratio = 0.5 * jnp.sinc(rotation_angle / (2.0 * jnp.pi)) ** 2
    torque = jnp.cross(fields, spins_now, axis=0)
    projection = lax.optimization_barrier(jnp.sum(fields * spins_now, axis=0))
    return cosine * spins_now + time_step * sine_ratio * torque + time_step * time_step * half_ratio * projection * fields

def reference(vectors, classical_spins, coefficients):

    def hamiltonian(states):
        neighbours = jnp.roll(states, 1, 2) + jnp.roll(states, -1, 2) + jnp.roll(states, 1, 3) + jnp.roll(states, -1, 3)
        return inverse_bound * (coupling * exchange_term(states, classical_spins) - hopping * neighbours)

    def one_block(block_index, summed):
        offset = block_index * R_DEV
        probes = lax.dynamic_slice_in_dim(vectors, offset, R_DEV, 1).astype(jnp.float32)
        previous = probes
        current = probes
        moments = coefficients[0] * probes
        for degree in range(STEPS):
            if degree == 0:
                following = hamiltonian(current)
            else:
                following = 2.0 * hamiltonian(current) - previous
            moments = moments + coefficients[degree + 1] * following
            previous, current = (current, following)
        return summed + spin_density(probes, moments)
    summed = lax.fori_loop(0, N_VEC, one_block, jnp.zeros((3, NX, NY), jnp.float32))
    fields = summed * (coupling / (R_DEV * N_VEC))
    return (rotate_spins(classical_spins, fields), fields)
```

```python
import functools

import jax
import jax.numpy as jnp
from jax import lax
from jax.experimental import pallas as pl
from jax.experimental.pallas import tpu as pltpu
from jax.sharding import PartitionSpec as P

coupling = 2.0
hopping = 1.0
inverse_bound = 1.0 / 6.5
time_step = 1.0

LANES = 8
REACH = 4
HALO = 2


def scale_of(coefs, count):
    step = -hopping * inverse_bound
    return 8.0 * coefs[4] * step**4 * (coupling / count)


def ratios(coefs):
    step = -hopping * inverse_bound
    c = [jnp.full((LANES, 128), coefs[k], jnp.float32) for k in range(5)]
    top = 1.0 / (c[4] * (8.0 * step**4))
    return [
        (c[0] - c[2] + c[4]) * top,
        (c[1] - 3.0 * c[3]) * step * top,
        (2.0 * c[2] - 8.0 * c[4]) * step**2 * top,
        4.0 * c[3] * step**3 * top,
    ]


def wide(row, width):
    return jnp.concatenate([row] * (width // 128), axis=1)


def sideways(state):
    return [pltpu.roll(x, 1, 1) + pltpu.roll(x, x.shape[1] - 1, 1) for x in state]


def plus(*states):
    return [functools.reduce(lambda a, b: a + b, parts) for parts in zip(*states)]


def on_site(state, spins, ratio=None):
    sx, sy, sz = spins
    ur, ui, dr, di = state
    zp, zm = (sz, sz) if ratio is None else (sz + ratio, sz - ratio)
    return [
        zp * ur + sx * dr + sy * di,
        zp * ui + sx * di - sy * dr,
        sx * ur - sy * ui - zm * dr,
        sx * ui + sy * ur - zm * di,
    ]


def flat(state, spins, ratio=None):
    return plus(sideways(state), on_site(state, spins, ratio))


def density(r, w):
    return [
        r[0] * w[2] + r[1] * w[3] + r[2] * w[0] + r[3] * w[1],
        r[0] * w[3] - r[1] * w[2] - r[2] * w[1] + r[3] * w[0],
        r[0] * w[0] + r[1] * w[1] - r[2] * w[2] - r[3] * w[3],
    ]


def times(ratio, state):
    return [ratio * x for x in state]


def load(ref, *at):
    return [ref[(*at, k)] for k in range(ref.shape[len(at)])]


def save(ref, at, state):
    for k, x in enumerate(state):
        ref[(*at, k)] = x


def unroll(v_ref, comp, rows_ref):
    tiles, length, _ = rows_ref.shape
    states = v_ref[comp].astype(jnp.float32).reshape(length, tiles * 128)
    for t in range(tiles):
        rows_ref[t] = states[:, t * 128 : (t + 1) * 128]


def row_of(rows_ref, y, rows):
    tiles = rows_ref.shape[0]
    return jnp.concatenate([rows_ref[t, pl.ds(y, LANES, stride=rows), :] for t in range(tiles)], axis=1)


def edges_kernel(v_ref, low_ref, high_ref, rows_ref):
    rows, width = v_ref.shape[2:]
    for comp in range(4):
        unroll(v_ref, comp, rows_ref)
        for i in range(HALO):
            low_ref[i, comp] = row_of(rows_ref, i, rows)
            high_ref[i, comp] = row_of(rows_ref, rows - 1 - i, rows)


def edge_rows(vectors):
    _, count, rows, width = vectors.shape
    out = jax.ShapeDtypeStruct((HALO, 4, count, width), jnp.float32)
    spec = pl.BlockSpec((HALO, 4, LANES, width), lambda g: (0, 0, g, 0))
    return pl.pallas_call(
        edges_kernel,
        grid=(count // LANES,),
        in_specs=[pl.BlockSpec((4, LANES, rows, width), lambda g: (0, g, 0, 0))],
        out_specs=[spec, spec],
        out_shape=[out, out],
        scratch_shapes=[pltpu.VMEM((width // 128, LANES * rows, 128), jnp.float32)],
        compiler_params=pltpu.CompilerParams(vmem_limit_bytes=24 << 20),
        name="edge_rows",
    )(vectors)


def inner_kernel(coef_ref, v_ref, s_ref, f_ref, low_ref, high_ref, rows_ref, r_ref, sp_ref, a_ref, b_ref, acc_ref):
    rows, width = v_ref.shape[2:]
    step = pl.program_id(0)
    last = pl.num_programs(0) - 1
    rho = [wide(x, width) for x in ratios(coef_ref)]
    field = -(coupling / hopping)

    @pl.when(step == 0)
    def _():
        for y in range(rows + 2):
            for k in range(3):
                sp_ref[y, k] = jnp.broadcast_to(s_ref[k, y : y + 1, :] * field, (LANES, width))

    for comp in range(4):
        unroll(v_ref, comp, rows_ref)
        for y in range(rows):
            r_ref[y, comp] = row_of(rows_ref, y, rows)
        for i in range(REACH):
            low_ref[i, comp] = r_ref[i, comp]
            high_ref[i, comp] = r_ref[rows - 1 - i, comp]

    save(a_ref, (1,), load(r_ref, 0))
    save(a_ref, (rows + 2,), load(r_ref, rows - 1))

    def one(y, above, below):
        here = load(r_ref, y)
        out = flat(here, load(sp_ref, y + 1), rho[3])
        for other in above + below:
            out = plus(out, load(r_ref, other))
        save(a_ref, (y + 2,), out)

    one(0, [], [1])

    @pl.loop(1, rows - 1)
    def _(y):
        one(y, [y - 1], [y + 1])

    one(rows - 1, [rows - 2], [])

    save(b_ref, (0,), load(a_ref, 1))
    save(b_ref, (rows + 3,), load(a_ref, rows + 2))
    save(b_ref, (1,), plus(flat(load(a_ref, 1), load(sp_ref, 0)), load(a_ref, 2)))
    save(b_ref, (rows + 2,), plus(flat(load(a_ref, rows + 2), load(sp_ref, rows + 1)), load(a_ref, rows + 1)))

    def further(src, y, ratio):
        here = load(src, y + 2)
        out = flat(here, load(sp_ref, y + 1))
        out = plus(out, load(src, y + 1), load(src, y + 3))
        if ratio is not None:
            out = plus(out, times(ratio, load(r_ref, y)))
        return out

    @pl.loop(0, rows)
    def _(y):
        save(b_ref, (y + 2,), further(a_ref, y, rho[2]))

    save(a_ref, (1,), further(b_ref, -1, None))
    save(a_ref, (rows + 2,), further(b_ref, rows, None))

    @pl.loop(0, rows)
    def _(y):
        save(a_ref, (y + 2,), further(b_ref, y, rho[1]))

    @pl.loop(0, rows)
    def _(y):
        here = density(load(r_ref, y), further(a_ref, y, rho[0]))

        @pl.when(step == 0)
        def _():
            save(acc_ref, (y,), here)

        @pl.when(step > 0)
        def _():
            save(acc_ref, (y,), plus(here, load(acc_ref, y)))

    @pl.when(step == last)
    def _():
        for y in range(rows):
            for k in range(3):
                f_ref[k, y : y + 1, :] = jnp.sum(acc_ref[y, k], axis=0, keepdims=True)


def inner(coefficients, vectors, spins):
    _, count, rows, width = vectors.shape
    edge = jax.ShapeDtypeStruct((REACH, 4, count, width), jnp.float32)
    edge_spec = pl.BlockSpec((REACH, 4, LANES, width), lambda g: (0, 0, g, 0))
    f32 = jnp.float32
    return pl.pallas_call(
        inner_kernel,
        grid=(count // LANES,),
        in_specs=[
            pl.BlockSpec(memory_space=pltpu.SMEM),
            pl.BlockSpec((4, LANES, rows, width), lambda g: (0, g, 0, 0)),
            pl.BlockSpec((3, rows + 2, width), lambda g: (0, 0, 0)),
        ],
        out_specs=[pl.BlockSpec((3, rows, width), lambda g: (0, 0, 0)), edge_spec, edge_spec],
        out_shape=[jax.ShapeDtypeStruct((3, rows, width), f32), edge, edge],
        scratch_shapes=[
            pltpu.VMEM((width // 128, LANES * rows, 128), f32),
            pltpu.VMEM((rows, 4, LANES, width), f32),
            pltpu.VMEM((rows + 2, 3, LANES, width), f32),
            pltpu.VMEM((rows + 4, 4, LANES, width), f32),
            pltpu.VMEM((rows + 4, 4, LANES, width), f32),
            pltpu.VMEM((rows, 3, LANES, width), f32),
        ],
        compiler_params=pltpu.CompilerParams(vmem_limit_bytes=48 << 20),
        cost_estimate=pl.CostEstimate(flops=240 * vectors.size, bytes_accessed=8 << 20, transcendentals=0),
        name="inner",
    )(coefficients, vectors, spins)


def outer_kernel(coef_ref, own_ref, halo_ref, s_ref, f_ref, g_ref, sp_ref, facc_ref, gacc_ref):
    width = own_ref.shape[-1]
    step = pl.program_id(1)
    last = pl.num_programs(1) - 1
    rho = [wide(x, width) for x in ratios(coef_ref)]
    field = -(coupling / hopping)

    @pl.when(step == 0)
    def _():
        for y in range(5):
            for k in range(3):
                sp_ref[y, k] = jnp.broadcast_to(s_ref[0, k, y : y + 1, :] * field, (LANES, width))

    def spin(name):
        return load(sp_ref, ("B2", "B1", "A1", "A2", "A3").index(name))

    own = lambda i: load(own_ref, 0, i - 1)
    halo = lambda j: load(halo_ref, 0, j - 1)
    b1, b2 = halo(1), halo(2)

    a_b2 = plus(flat(b2, spin("B2"), rho[3]), b1)
    a_b1 = plus(flat(b1, spin("B1"), rho[3]), b2)
    b_b2 = plus(flat(a_b2, spin("B2")), a_b1, b2, times(rho[2], b2))
    b_b1 = plus(flat(a_b1, spin("B1")), a_b2, b1, times(rho[2], b1))
    b_a1 = plus(flat(b1, spin("A1")), a_b1)
    c_b1 = plus(flat(b_b1, spin("B1")), b_b2, b_a1, times(rho[1], b1))
    c_a1 = plus(flat(b_a1, spin("A1")), b_b1, b1)
    c_a2 = plus(flat(b1, spin("A2")), b_a1)
    w = [
        plus(flat(c_a1, spin("A1")), c_b1, c_a2),
        plus(flat(c_a2, spin("A2")), c_a1, b1),
        plus(flat(b1, spin("A3")), c_a2),
        b1,
    ]
    f = [density(own(i + 1), w[i]) for i in range(REACH)]
    a3 = own(3)
    spins = plus(*[spin(name) for name in ("A3", "A2", "A1", "B1")])
    w_b1 = plus(on_site(a3, spins, rho[3]), times(4.0, sideways(a3)), own(4))
    g = [density(b1, w_b1), density(b2, a3)]

    @pl.when(step == 0)
    def _():
        for i, x in enumerate(f):
            save(facc_ref, (i,), x)
        for i, x in enumerate(g):
            save(gacc_ref, (i,), x)

    @pl.when(step > 0)
    def _():
        for i, x in enumerate(f):
            save(facc_ref, (i,), plus(x, load(facc_ref, i)))
        for i, x in enumerate(g):
            save(gacc_ref, (i,), plus(x, load(gacc_ref, i)))

    @pl.when(step == last)
    def _():
        for acc, out, n in ((facc_ref, f_ref, REACH), (gacc_ref, g_ref, HALO)):
            for i in range(n):
                for k in range(3):
                    out[0, k, i : i + 1, :] = jnp.sum(acc[i, k], axis=0, keepdims=True)


def outer(coefficients, own, halo, spins):
    _, _, _, count, width = own.shape
    f32 = jnp.float32
    return pl.pallas_call(
        outer_kernel,
        grid=(2, count // LANES),
        in_specs=[
            pl.BlockSpec(memory_space=pltpu.SMEM),
            pl.BlockSpec((1, REACH, 4, LANES, width), lambda e, g: (e, 0, 0, g, 0)),
            pl.BlockSpec((1, HALO, 4, LANES, width), lambda e, g: (e, 0, 0, g, 0)),
            pl.BlockSpec((1, 3, 5, width), lambda e, g: (e, 0, 0, 0)),
        ],
        out_specs=[
            pl.BlockSpec((1, 3, REACH, width), lambda e, g: (e, 0, 0, 0)),
            pl.BlockSpec((1, 3, HALO, width), lambda e, g: (e, 0, 0, 0)),
        ],
        out_shape=[
            jax.ShapeDtypeStruct((2, 3, REACH, width), f32),
            jax.ShapeDtypeStruct((2, 3, HALO, width), f32),
        ],
        scratch_shapes=[
            pltpu.VMEM((5, 3, LANES, width), f32),
            pltpu.VMEM((REACH, 3, LANES, width), f32),
            pltpu.VMEM((HALO, 3, LANES, width), f32),
        ],
        compiler_params=pltpu.CompilerParams(vmem_limit_bytes=48 << 20),
        cost_estimate=pl.CostEstimate(flops=80 * own.size, bytes_accessed=4 << 20, transcendentals=0),
        name="outer",
    )(coefficients, own, halo, spins)


def rotate_spins(spins_now, fields):
    magnitude = jnp.sqrt(jnp.sum(fields * fields, axis=0))
    rotation_angle = time_step * magnitude
    cosine = jnp.cos(rotation_angle)
    sine_ratio = jnp.sinc(rotation_angle / jnp.pi)
    half_ratio = 0.5 * jnp.sinc(rotation_angle / (2.0 * jnp.pi)) ** 2
    torque = jnp.cross(fields, spins_now, axis=0)
    projection = jnp.sum(fields * spins_now, axis=0)
    return (
        cosine * spins_now
        + time_step * sine_ratio * torque
        + time_step * time_step * half_ratio * projection * fields
    )


def summed_over(part, axis):
    count = lax.axis_size(axis)
    if count & (count - 1):
        return lax.psum(part, axis)
    apart = 1
    while apart < count:
        part = part + lax.ppermute(part, axis, [(i, i ^ apart) for i in range(count)])
        apart *= 2
    return part


def shards(vectors, classical_spins, coefficients):
    count_all = vectors.shape[1] * lax.axis_size("vec")
    rows = vectors.shape[2]
    number = lax.axis_size("lat")
    forward = [(i, (i + 1) % number) for i in range(number)]
    backward = [(b, a) for a, b in forward]
    down = lambda x: lax.ppermute(x, "lat", forward)
    up = lambda x: lax.ppermute(x, "lat", backward)

    spin_low = down(classical_spins[:, rows - HALO :])
    spin_high = up(classical_spins[:, :HALO])
    low, high = edge_rows(vectors)
    halo_low, halo_high = down(high), up(low)

    spins_wide = jnp.concatenate([spin_low, classical_spins, spin_high], axis=1)
    f_in, own_low, own_high = inner(coefficients, vectors, spins_wide[:, HALO - 1 : rows + HALO + 1])
    own = jnp.stack([own_low, own_high])
    spin_edges = jnp.stack([spins_wide[:, :5], jnp.flip(spins_wide[:, -5:], 1)])
    f_out, g_out = outer(coefficients, own, jnp.stack([halo_low, halo_high]), spin_edges)

    total = f_in.at[:, :REACH].add(f_out[0]).at[:, rows - REACH :].add(jnp.flip(f_out[1], 1))
    total, given = summed_over((total), "vec"), summed_over(g_out, "vec")
    from_low, from_high = down(given[1]), up(given[0])
    total = total.at[:, :HALO].add(from_low).at[:, rows - HALO :].add(jnp.flip(from_high, 1))
    fields = total * scale_of(coefficients, count_all)
    return rotate_spins(classical_spins, fields), fields


def solution(mesh):
    placed = (P(None, "vec", "lat", None), P(None, "lat", None), P())
    return jax.shard_map(
        shards,
        mesh=mesh,
        in_specs=placed,
        out_specs=(P(None, "lat", None), P(None, "lat", None)),
        check_vma=False,
    )
```

```python
import functools

import jax
import jax.numpy as jnp
from jax import lax
from jax.experimental import pallas as pl
from jax.experimental.pallas import tpu as pltpu
from jax.sharding import PartitionSpec as P

coupling = 2.0
hopping = 1.0
inverse_bound = 1.0 / 6.5
time_step = 1.0

LANES = 8
REACH = 4
HALO = 2
MIB = 1 << 20


def ratios(coefs):
    step = -hopping * inverse_bound
    c = [jnp.full((LANES, 128), coefs[k], jnp.float32) for k in range(5)]
    top = c[4] * (8.0 * step**4)
    under = 1.0 / top
    return [
        (c[0] - c[2] + c[4]) * under,
        (c[1] - 3.0 * c[3]) * step * under,
        (2.0 * c[2] - 8.0 * c[4]) * step**2 * under,
        4.0 * c[3] * step**3 * under,
        top,
    ]


def block_of(width):
    return next(b for b in (512, 256, 128) if width % b == 0)


def shuffle(width, back=False):
    block = block_of(width)
    tiles = block // 128
    source = lax.broadcasted_iota(jnp.int32, (block, block), 1 if back else 0)
    target = lax.broadcasted_iota(jnp.int32, (block, block), 0 if back else 1)
    place = lax.rem(source, tiles) * 128 + lax.div(source, tiles)
    return (place == target).astype(jnp.float32).astype(jnp.bfloat16)


def moved(states, matrix):
    block = matrix.shape[0]
    out = []
    for at in range(0, states.shape[1], block):
        got = jnp.dot(states[:, at : at + block], matrix, preferred_element_type=jnp.float32)
        out += [got[:, t : t + 128] for t in range(0, block, 128)]
    return out


def moved_exactly(rows, matrix):
    parts = []
    for _ in range(3):
        parts.append(rows.astype(jnp.bfloat16))
        rows = rows - parts[-1].astype(jnp.float32)
    count = rows.shape[0]
    got = moved(jnp.concatenate(parts, axis=0), matrix)
    return [x[:count] + x[count : 2 * count] + x[2 * count :] for x in got]


def beside(tiles):
    count = len(tiles)
    group = block_of(count * 128) // 128
    blocks = count // group
    lane = lax.broadcasted_iota(jnp.int32, tiles[0].shape, 1)
    ends = [pltpu.roll(tiles[b * group + group - 1], 1, 1) for b in range(blocks)]
    starts = [pltpu.roll(tiles[b * group], 127, 1) for b in range(blocks)]
    out = []
    for b in range(blocks):
        left = ends[b] if blocks == 1 else jnp.where(lane == 0, ends[b - 1], ends[b])
        right = starts[b] if blocks == 1 else jnp.where(lane == 127, starts[(b + 1) % blocks], starts[b])
        for t in range(group):
            at = b * group + t
            out.append((left if t == 0 else tiles[at - 1]) + (right if t == group - 1 else tiles[at + 1]))
    return out


def on_site(state, spins, ratio=None):
    sx, sy, sz = spins
    ur, ui, dr, di = state
    zp, zm = (sz, sz) if ratio is None else (sz + ratio, sz - ratio)
    return [
        zp * ur + sx * dr + sy * di,
        zp * ui + sx * di - sy * dr,
        sx * ur - sy * ui - zm * dr,
        sx * ui + sy * ur - zm * di,
    ]


def density(r, w):
    return [
        r[0] * w[2] + r[1] * w[3] + r[2] * w[0] + r[3] * w[1],
        r[0] * w[3] - r[1] * w[2] - r[2] * w[1] + r[3] * w[0],
        r[0] * w[0] + r[1] * w[1] - r[2] * w[2] - r[3] * w[3],
    ]


def plus(*states):
    return [functools.reduce(lambda a, b: a + b, parts) for parts in zip(*states)]


def times(ratio, state):
    return [ratio * x for x in state]


def load(ref, at, t):
    return [ref[(*at, k, slice(None), pl.ds(t * 128, 128))] for k in range(ref.shape[len(at)])]


def save(ref, at, t, state):
    for k, x in enumerate(state):
        ref[(*at, k, slice(None), pl.ds(t * 128, 128))] = x


def by_tile(row):
    ref, at = row
    return [load(ref, at, t) for t in range(ref.shape[-1] // 128)]


def flat(row, spin, ratio=None):
    sides = [beside([x[k] for x in row]) for k in range(4)]
    for t, here in enumerate(row):
        yield t, plus([x[t] for x in sides], on_site(here, load(*spin, t), ratio))


def side_by_side(tiles):
    sub = lax.broadcasted_iota(jnp.int32, tiles[0].shape, 0)
    apart = 4
    while apart:
        first = (sub & apart) == 0
        tiles = [
            jnp.where(first, x + pltpu.roll(x, 8 - apart, 0), y + pltpu.roll(y, apart, 0))
            for x, y in zip(tiles[: len(tiles) // 2], tiles[len(tiles) // 2 :])
        ]
        apart //= 2
    return tiles[0]


def edges_kernel(v_hbm, s_hbm, low_ref, high_ref, v_ref, s_ref, rows_ref, v_sem, s_sem):
    _, count, rows, width = v_hbm.shape
    copies = {}
    for comp in range(4):
        for g in range(count // LANES):
            at = pl.ds(g * LANES, LANES)
            copies[g, comp] = pltpu.make_async_copy(v_hbm.at[comp, at], v_ref.at[g, comp], v_sem.at[g, comp])
            copies[g, comp].start()
    spins = pltpu.make_async_copy(s_hbm, s_ref, s_sem)
    spins.start()
    for (g, comp), copy in copies.items():
        copy.wait()
        states = v_ref[g, comp].astype(jnp.float32).reshape(LANES * rows, width)
        for t in range(width // 128):
            rows_ref[comp, t] = states[:, t * 128 : (t + 1) * 128]
        for i in range(HALO):
            to = pl.ds((i * 4 + comp) * count + g * LANES, LANES)
            for t in range(width // 128):
                at = pl.ds(t * 128, 128)
                low_ref[to, at] = rows_ref[comp, t, pl.ds(i, LANES, stride=rows), :]
                high_ref[to, at] = rows_ref[comp, t, pl.ds(rows - 1 - i, LANES, stride=rows), :]
    spins.wait()
    end = HALO * 4 * count
    for ref, at in ((low_ref, lambda i: i), (high_ref, lambda i: rows - 1 - i)):
        lines = [s_ref[k, at(i) : at(i) + 1] for k in range(3) for i in range(HALO)]
        ref[end:] = jnp.concatenate(lines + lines[:2], axis=0)


def edges(vectors, spins):
    _, count, rows, width = vectors.shape
    f32 = jnp.float32
    out = jax.ShapeDtypeStruct((HALO * 4 * count + 8, width), f32)
    return pl.pallas_call(
        edges_kernel,
        in_specs=[pl.BlockSpec(memory_space=pl.ANY)] * 2,
        out_shape=[out] * 2,
        scratch_shapes=[
            pltpu.VMEM((count // LANES, 4, LANES, rows, width), jnp.bfloat16),
            pltpu.VMEM(spins.shape, f32),
            pltpu.VMEM((4, width // 128, LANES * rows, 128), f32),
            pltpu.SemaphoreType.DMA((count // LANES, 4)),
            pltpu.SemaphoreType.DMA,
        ],
        compiler_params=pltpu.CompilerParams(vmem_limit_bytes=56 * MIB),
        name="edges",
    )(vectors, spins)


KEPT = REACH + 2


def inner_kernel(coef_ref, v_ref, s_ref, f_ref, kept_ref, rows_ref, r_ref, sp_ref, a_ref, b_ref, acc_ref, mat_ref):
    _, _, rows, width = v_ref.shape
    tiles = width // 128
    step = pl.program_id(0)
    last = pl.num_programs(0) - 1
    rho = ratios(coef_ref)

    @pl.when(step == 0)
    def _():
        mat_ref[...] = shuffle(width)
        acc_ref[...] = jnp.zeros_like(acc_ref)
        spins = s_ref[...].reshape(3 * rows, width) * -(coupling / hopping)
        for t, got in enumerate(moved_exactly(spins, mat_ref[...])):
            for y in range(rows):
                for k in range(3):
                    row = got[k * rows + y : k * rows + y + 1]
                    sp_ref[y, k, :, t * 128 : (t + 1) * 128] = jnp.broadcast_to(row, (LANES, 128))

    for t, got in enumerate(moved(v_ref[...].reshape(4 * LANES * rows, width), mat_ref[...])):
        rows_ref[t] = got
    for y in range(rows):
        for comp in range(4):
            for t in range(tiles):
                at = pl.ds(comp * LANES * rows + y, LANES, stride=rows)
                r_ref[y, comp, :, t * 128 : (t + 1) * 128] = rows_ref[t, at, :]

    def apply(dst, src, y, others, ratio, own):
        here = by_tile((src, (y,)))
        for t, x in flat(here, (sp_ref, (y,)), ratio if own else None):
            for o in others:
                x = plus(x, load(src, (o,), t))
            if not own:
                x = plus(x, times(ratio, load(r_ref, (y,), t)))
            dst(y, t, x)

    def pass_over(dst, src, ratio, own=False):
        apply(dst, src, 0, [1], ratio, own)
        apply(dst, src, rows - 1, [rows - 2], ratio, own)

        @pl.loop(1, rows - 1, unroll=2)
        def _(y):
            apply(dst, src, y, [y - 1, y + 1], ratio, own)

    def into(ref):
        return lambda y, t, x: save(ref, (y,), t, x)

    def fields(y, t, w):
        save(acc_ref, (y,), t, plus(density(load(r_ref, (y,), t), w), load(acc_ref, (y,), t)))

    pass_over(into(a_ref), r_ref, rho[3], own=True)
    pass_over(into(b_ref), a_ref, rho[2])
    for e in range(2):
        for i in range(REACH):
            kept_ref[0, e, i] = r_ref[rows - 1 - i if e else i]
        kept_ref[0, e, REACH] = a_ref[rows - 1 if e else 0]
        kept_ref[0, e, REACH + 1] = b_ref[rows - 1 if e else 0]
    pass_over(into(a_ref), b_ref, rho[1])
    pass_over(fields, a_ref, rho[0])

    @pl.when(step == last)
    def _():
        for k in range(3):
            for y in range(0, rows, 8):
                for t in range(tiles):
                    at = pl.ds(t * 128, 128)
                    f_ref[k, y : y + 8, at] = side_by_side([acc_ref[y + i, k, :, at] for i in range(8)])


def inner(coefficients, vectors, spins):
    _, count, rows, width = vectors.shape
    f32 = jnp.float32
    kept = (2, KEPT, 4, LANES, width)
    state = pltpu.VMEM((rows, 4, LANES, width), f32)
    return pl.pallas_call(
        inner_kernel,
        grid=(count // LANES,),
        in_specs=[
            pl.BlockSpec(memory_space=pltpu.SMEM),
            pl.BlockSpec((4, LANES, rows, width), lambda g: (0, g, 0, 0)),
            pl.BlockSpec((3, rows, width), lambda g: (0, 0, 0)),
        ],
        out_specs=[
            pl.BlockSpec((3, rows, width), lambda g: (0, 0, 0)),
            pl.BlockSpec((1, *kept), lambda g: (g, 0, 0, 0, 0, 0)),
        ],
        out_shape=[
            jax.ShapeDtypeStruct((3, rows, width), f32),
            jax.ShapeDtypeStruct((count // LANES, *kept), f32),
        ],
        scratch_shapes=[
            pltpu.VMEM((width // 128, 4 * LANES * rows, 128), f32),
            state,
            pltpu.VMEM((rows, 3, LANES, width), f32),
            state,
            state,
            pltpu.VMEM((rows, 3, LANES, width), f32),
            pltpu.VMEM((block_of(width),) * 2, jnp.bfloat16),
        ],
        compiler_params=pltpu.CompilerParams(vmem_limit_bytes=40 * MIB),
        cost_estimate=pl.CostEstimate(flops=240 * vectors.size, bytes_accessed=8 * MIB, transcendentals=0),
        name="inner",
    )(coefficients, vectors, spins)


SPINS = ("B2", "B1", "A1", "A2", "A3", "B1 to A3")


def given_kernel(coef_ref, kept_ref, low_ref, high_ref, s_ref, sp_ref, halo_ref, g_low_ref, g_high_ref):
    _, rows, width = s_ref.shape
    parts = kept_ref.shape[0]
    count = parts * LANES
    tiles = width // 128
    end = HALO * 4 * count
    rho = ratios(coef_ref)
    matrix = shuffle(width)
    lines = []
    for e, ref in enumerate((low_ref, high_ref)):
        for k in range(3):
            at = end + k * HALO
            lines += [ref[at + 1 : at + 2], ref[at : at + 1]]
            lines += [s_ref[k, y : y + 1] for y in ([rows - 1, rows - 2, rows - 3] if e else [0, 1, 2])]
    lines = jnp.concatenate(lines + lines[:2], axis=0) * -(coupling / hopping)
    for t, got in enumerate(moved_exactly(lines, matrix)):
        at = pl.ds(t * 128, 128)
        for e in range(2):
            for k in range(3):
                five = [got[(e * 3 + k) * 5 + i : (e * 3 + k) * 5 + i + 1] for i in range(5)]
                for i, row in enumerate(five + [five[1] + five[2] + five[3] + five[4]]):
                    sp_ref[e, i, k, :, at] = jnp.broadcast_to(row, (LANES, 128))
    for e, ref in enumerate((low_ref, high_ref)):
        for t, got in enumerate(moved(ref[:end].astype(jnp.bfloat16), matrix)):
            got = got.reshape(HALO, 4, parts, LANES, 128)
            for g in range(parts):
                halo_ref[g, e, :, :, :, t * 128 : (t + 1) * 128] = got[:, :, g]

    for e, ref in enumerate((g_low_ref, g_high_ref)):
        sums = [None] * tiles
        for g in range(parts):
            own = lambda i: (kept_ref, (g, e, i - 1))
            b1, b2 = (halo_ref, (g, e, 0)), (halo_ref, (g, e, 1))
            a3 = by_tile(own(3))
            sides = [beside([x[k] for x in a3]) for k in range(4)]
            for t in range(tiles):
                w = on_site(a3[t], load(sp_ref, (e, SPINS.index("B1 to A3")), t), rho[3])
                w = plus(w, times(4.0, [x[t] for x in sides]), load(*own(4), t))
                here = density(load(*b1, t), w) + density(load(*b2, t), a3[t])
                sums[t] = here if g == 0 else plus(sums[t], here)
        for t, x in enumerate(sums):
            rows_out = [x[i * 3 + k] for k in range(3) for i in range(HALO)]
            ref[:, t * 128 : (t + 1) * 128] = side_by_side(rows_out + rows_out[:2])


def given(coefficients, kept, low, high, spins):
    f32 = jnp.float32
    parts, width = kept.shape[0], spins.shape[-1]
    out = [(2, len(SPINS), 3, LANES, width), (parts, 2, HALO, 4, LANES, width), (8, width), (8, width)]
    vmem = pl.BlockSpec(memory_space=pltpu.VMEM)
    return pl.pallas_call(
        given_kernel,
        in_specs=[pl.BlockSpec(memory_space=pltpu.SMEM)] + [vmem] * 4,
        out_specs=[vmem] * len(out),
        out_shape=[jax.ShapeDtypeStruct(x, f32) for x in out],
        compiler_params=pltpu.CompilerParams(vmem_limit_bytes=32 * MIB),
        cost_estimate=pl.CostEstimate(flops=100 * low.size, bytes_accessed=4 * MIB, transcendentals=0),
        name="given",
    )(coefficients, kept, low, high, spins)


def outer_kernel(begin, end, part, coef_ref, kept_ref, sp_ref, halo_ref, *refs):
    width = halo_ref.shape[-1]
    tiles = width // 128
    rho = ratios(coef_ref)
    before = None if begin else refs[0]
    refs = refs if begin else refs[1:]
    if end:
        f_ref, below_ref, above_ref, out_ref, mid_ref, acc_ref = refs
    else:
        acc_ref, mid_ref = refs

    @pl.loop(0, 2)
    def _(e):
        spin = lambda name: (sp_ref, (e, SPINS.index(name)))
        own = lambda i: (kept_ref, (part, e, i - 1))
        a_in, b_in = (kept_ref, (part, e, REACH)), (kept_ref, (part, e, REACH + 1))
        b1, b2 = (halo_ref, (part, e, 0)), (halo_ref, (part, e, 1))
        names = ("a_b2", "a_b1", "b_b2", "b_b1", "b_a1", "c_b1", "c_a1", "c_a2")
        mid = {name: (mid_ref, (i,)) for i, name in enumerate(names)}

        def make(row, at, others, ratio=None, extra=None):
            for t, x in flat(by_tile(row), spin(at), ratio):
                for ref, place in others:
                    x = plus(x, load(ref, place, t))
                if extra is not None:
                    x = plus(x, times(extra[0], load(*extra[1], t)))
                yield t, x

        def state(name, *rest, **more):
            for t, x in make(*rest, **more):
                save(*mid[name], t, x)

        def fields(i, r, w):
            for t, x in w:
                x = density(load(*r, t), x)
                if before is not None:
                    x = plus(x, load(before, (e, i), t))
                save(acc_ref, (e, i), t, x)

        state("a_b2", b2, "B2", [b1], ratio=rho[3])
        state("a_b1", b1, "B1", [b2, own(1)], ratio=rho[3])
        state("b_b2", mid["a_b2"], "B2", [mid["a_b1"], b2], extra=(rho[2], b2))
        state("b_b1", mid["a_b1"], "B1", [mid["a_b2"], a_in, b1], extra=(rho[2], b1))
        state("b_a1", b1, "A1", [mid["a_b1"]])
        state("c_b1", mid["b_b1"], "B1", [mid["b_b2"], b_in, mid["b_a1"]], extra=(rho[1], b1))
        state("c_a1", mid["b_a1"], "A1", [mid["b_b1"], b1])
        state("c_a2", b1, "A2", [mid["b_a1"]])
        fields(0, own(1), make(mid["c_a1"], "A1", [mid["c_b1"], mid["c_a2"]]))
        fields(1, own(2), make(mid["c_a2"], "A2", [mid["c_a1"], b1]))
        fields(2, own(3), make(b1, "A3", [mid["c_a2"]]))
        fields(3, own(4), ((t, load(*b1, t)) for t in range(tiles)))

    if end:
        rows = f_ref.shape[1]
        out_ref[...] = f_ref[...]
        half = lax.broadcasted_iota(jnp.int32, (8, 128), 0) < REACH
        for t in range(tiles):
            at = pl.ds(t * 128, 128)
            for k in range(3):
                low = [acc_ref[0, i, k, :, at] for i in range(REACH)]
                high = [acc_ref[1, i, k, :, at] for i in reversed(range(REACH))]
                edge = side_by_side(low + high)
                out_ref[k, :8, at] += jnp.where(half, edge, 0.0)
                out_ref[k, rows - 8 :, at] += jnp.where(half, 0.0, edge)
        for k in range(3):
            for i in range(HALO):
                line = k * HALO + i
                out_ref[k, i : i + 1] += below_ref[line : line + 1]
                out_ref[k, rows - 1 - i : rows - i] += above_ref[line : line + 1]


def outer(coefficients, kept, sp, halo, part, so_far, rest):
    parts, width = kept.shape[0], kept.shape[-1]
    f32 = jnp.float32
    begin, end = part == 0, part == parts - 1
    acc, mid = (2, REACH, 3, LANES, width), (8, 4, LANES, width)
    more = ([] if begin else [so_far]) + (list(rest) if end else [])
    vmem = pl.BlockSpec(memory_space=pltpu.VMEM)
    return pl.pallas_call(
        functools.partial(outer_kernel, begin, end, part),
        in_specs=[pl.BlockSpec(memory_space=pltpu.SMEM)] + [vmem] * (3 + len(more)),
        out_specs=vmem,
        out_shape=jax.ShapeDtypeStruct(rest[0].shape if end else acc, f32),
        scratch_shapes=[pltpu.VMEM(mid, f32)] + ([pltpu.VMEM(acc, f32)] if end else []),
        compiler_params=pltpu.CompilerParams(vmem_limit_bytes=32 * MIB),
        cost_estimate=pl.CostEstimate(flops=300 * kept.size, bytes_accessed=3 * MIB, transcendentals=0),
        name="outer",
    )(coefficients, kept, sp, halo, *more)


def final_kernel(count_all, coef_ref, s_ref, f_ref, other_ref, rotated_ref, fields_ref):
    _, rows, width = s_ref.shape
    total = f_ref[...] + other_ref[...]
    scale = ratios(coef_ref)[4][:1, :1] * (coupling / count_all)
    got = moved_exactly(total.reshape(3 * rows, width), shuffle(width, back=True))
    for t, x in enumerate(got):
        at = pl.ds(t * 128, 128)
        field = [x[k * rows : (k + 1) * rows] * scale for k in range(3)]
        spin = [s_ref[k, :, at] for k in range(3)]
        size = jnp.sqrt(field[0] * field[0] + field[1] * field[1] + field[2] * field[2])
        half_angle = (0.5 * time_step) * size
        sine, cosine = jnp.sin(half_angle), jnp.cos(half_angle)
        some = half_angle > 0.0
        ratio = jnp.where(some, sine / jnp.where(some, half_angle, 1.0), 1.0)
        along = field[0] * spin[0] + field[1] * spin[1] + field[2] * spin[2]
        keep = 1.0 - 2.0 * sine * sine
        turn = time_step * ratio * cosine
        lift = (0.5 * time_step * time_step) * ratio * ratio * along
        for k in range(3):
            i, j = (k + 1) % 3, (k + 2) % 3
            cross = field[i] * spin[j] - field[j] * spin[i]
            rotated_ref[k, :, at] = keep * spin[k] + turn * cross + lift * field[k]
            fields_ref[k, :, at] = field[k]


def final(coefficients, spins, count_all, f, other):
    out = jax.ShapeDtypeStruct(spins.shape, jnp.float32)
    vmem = pl.BlockSpec(memory_space=pltpu.VMEM)
    return pl.pallas_call(
        functools.partial(final_kernel, count_all),
        in_specs=[pl.BlockSpec(memory_space=pltpu.SMEM)] + [vmem] * 3,
        out_specs=[vmem] * 2,
        out_shape=[out, out],
        compiler_params=pltpu.CompilerParams(vmem_limit_bytes=32 * MIB),
        name="final",
    )(coefficients, spins, f, other)


def shards(vectors, classical_spins, coefficients):
    across, number = lax.axis_size("vec"), lax.axis_size("lat")
    count_all = vectors.shape[1] * across
    parts = vectors.shape[1] // LANES

    def to_row(x, on):
        return lax.ppermute(x, "lat", [(i, (i + on) % number) for i in range(number)])

    def swap(x, step):
        steps = across.bit_length() - 1
        bit = lambda i: 1 << (step if i % 2 == 0 else steps - 1 - step)
        pairs = [(i * across + j, i * across + (j ^ bit(i))) for i in range(number) for j in range(across)]
        return lax.ppermute(x, ("lat", "vec"), pairs)

    low, high = edges(vectors, classical_spins)
    from_below, from_above = to_row(high, 1), to_row(low, -1)
    f, kept = inner(coefficients, vectors, classical_spins)
    sp, halo, g_low, g_high = given(coefficients, kept, from_below, from_above, classical_spins)
    below, above = to_row(g_high, 1), to_row(g_low, -1)
    so_far = None
    for part in range(parts):
        so_far = outer(coefficients, kept, sp, halo, part, so_far, (f, below, above))
    steps = across.bit_length() - 1
    if across != 1 << steps or steps == 0:
        return final(coefficients, classical_spins, count_all, lax.psum(so_far, "vec"), jnp.zeros_like(so_far))
    for step in range(steps - 1):
        so_far = so_far + swap(so_far, step)
    return final(coefficients, classical_spins, count_all, so_far, swap(so_far, steps - 1))


def solution(mesh):
    placed = (P(None, "vec", "lat", None), P(None, "lat", None), P())
    return jax.shard_map(
        shards,
        mesh=mesh,
        in_specs=placed,
        out_specs=(P(None, "lat", None), P(None, "lat", None)),
        check_vma=False,
    )
```

```python
import functools

import jax
import jax.numpy as jnp
from jax import lax
from jax.experimental import pallas as pl
from jax.experimental.pallas import tpu as pltpu
from jax.sharding import PartitionSpec as P

coupling = 2.0
hopping = 1.0
inverse_bound = 1.0 / 6.5
time_step = 1.0

LANES = 8
REACH = 4
HALO = 2
MIB = 1 << 20


def ratios(coefs):
    step = -hopping * inverse_bound
    c = [jnp.full((LANES, 128), coefs[k], jnp.float32) for k in range(5)]
    top = c[4] * (8.0 * step**4)
    under = 1.0 / top
    return [
        (c[0] - c[2] + c[4]) * under,
        (c[1] - 3.0 * c[3]) * step * under,
        (2.0 * c[2] - 8.0 * c[4]) * step**2 * under,
        4.0 * c[3] * step**3 * under,
        top,
    ]


def block_of(width):
    return next(b for b in (512, 256, 128) if width % b == 0)


def shuffle(width, back=False):
    block = block_of(width)
    tiles = block // 128
    source = lax.broadcasted_iota(jnp.int32, (block, block), 1 if back else 0)
    target = lax.broadcasted_iota(jnp.int32, (block, block), 0 if back else 1)
    place = lax.rem(source, tiles) * 128 + lax.div(source, tiles)
    return (place == target).astype(jnp.float32).astype(jnp.bfloat16)


def moved(states, matrix):
    block = matrix.shape[0]
    out = []
    for at in range(0, states.shape[1], block):
        got = jnp.dot(states[:, at : at + block], matrix, preferred_element_type=jnp.float32)
        out += [got[:, t : t + 128] for t in range(0, block, 128)]
    return out


def moved_exactly(rows, matrix):
    parts = []
    for _ in range(3):
        parts.append(rows.astype(jnp.bfloat16))
        rows = rows - parts[-1].astype(jnp.float32)
    count = rows.shape[0]
    got = moved(jnp.concatenate(parts, axis=0), matrix)
    return [x[:count] + x[count : 2 * count] + x[2 * count :] for x in got]


def on_left(tiles):
    group = block_of(len(tiles) * 128) // 128
    lane = lax.broadcasted_iota(jnp.int32, tiles[0].shape, 1)
    ends = [pltpu.roll(x, 1, 1) for x in tiles[group - 1 :: group]]
    if len(ends) > 1:
        ends = [jnp.where(lane == 0, ends[b - 1], x) for b, x in enumerate(ends)]
    return [tiles[t - 1] if t % group else ends[t // group] for t in range(len(tiles))]


def on_right(tiles):
    group = block_of(len(tiles) * 128) // 128
    lane = lax.broadcasted_iota(jnp.int32, tiles[0].shape, 1)
    starts = [pltpu.roll(x, 127, 1) for x in tiles[::group]]
    if len(starts) > 1:
        starts = [jnp.where(lane == 127, starts[(b + 1) % len(starts)], x) for b, x in enumerate(starts)]
    return [tiles[t + 1] if (t + 1) % group else starts[t // group] for t in range(len(tiles))]


def beside(tiles):
    return [x + y for x, y in zip(on_left(tiles), on_right(tiles))]


def on_site(state, spins, ratio=None):
    sx, sy, sz = spins
    ur, ui, dr, di = state
    zp, zm = (sz, sz) if ratio is None else (sz + ratio, sz - ratio)
    return [
        zp * ur + sx * dr + sy * di,
        zp * ui + sx * di - sy * dr,
        sx * ur - sy * ui - zm * dr,
        sx * ui + sy * ur - zm * di,
    ]


def density(r, w):
    return [
        r[0] * w[2] + r[1] * w[3] + r[2] * w[0] + r[3] * w[1],
        r[0] * w[3] - r[1] * w[2] - r[2] * w[1] + r[3] * w[0],
        r[0] * w[0] + r[1] * w[1] - r[2] * w[2] - r[3] * w[3],
    ]


def plus(*states):
    return [functools.reduce(lambda a, b: a + b, parts) for parts in zip(*states)]


def times(ratio, state):
    return [ratio * x for x in state]


def load(ref, at, t):
    return [ref[(*at, k, slice(None), pl.ds(t * 128, 128))] for k in range(ref.shape[len(at)])]


def save(ref, at, t, state):
    for k, x in enumerate(state):
        ref[(*at, k, slice(None), pl.ds(t * 128, 128))] = x


def by_tile(row):
    ref, at = row
    return [load(ref, at, t) for t in range(ref.shape[-1] // 128)]


def flat(row, spin, ratio=None):
    sides = [beside([x[k] for x in row]) for k in range(4)]
    for t, here in enumerate(row):
        yield t, plus([x[t] for x in sides], on_site(here, load(*spin, t), ratio))


def side_by_side(tiles):
    sub = lax.broadcasted_iota(jnp.int32, tiles[0].shape, 0)
    apart = 4
    while apart:
        first = (sub & apart) == 0
        tiles = [
            jnp.where(first, x + pltpu.roll(x, 8 - apart, 0), y + pltpu.roll(y, apart, 0))
            for x, y in zip(tiles[: len(tiles) // 2], tiles[len(tiles) // 2 :])
        ]
        apart //= 2
    return tiles[0]


def edges_kernel(v_ref, s_ref, low_ref, high_ref, rows_ref):
    _, count, rows, width = v_ref.shape
    for comp in range(4):
        for g in range(count // LANES):
            states = v_ref[comp, g * LANES : (g + 1) * LANES].astype(jnp.float32).reshape(LANES * rows, width)
            for t in range(width // 128):
                rows_ref[comp, g, t] = states[:, t * 128 : (t + 1) * 128]
            for i in range(HALO):
                to = pl.ds((i * 4 + comp) * count + g * LANES, LANES)
                for t in range(width // 128):
                    at = pl.ds(t * 128, 128)
                    low_ref[to, at] = rows_ref[comp, g, t, pl.ds(i, LANES, stride=rows), :]
                    high_ref[to, at] = rows_ref[comp, g, t, pl.ds(rows - 1 - i, LANES, stride=rows), :]
    end = HALO * 4 * count
    low_ref[end:] = s_ref[0]
    high_ref[end:] = s_ref[1]


def edges(vectors, spin_lines):
    _, count, rows, width = vectors.shape
    f32 = jnp.float32
    out = jax.ShapeDtypeStruct((HALO * 4 * count + 8, width), f32)
    vmem = pl.BlockSpec(memory_space=pltpu.VMEM)
    return pl.pallas_call(
        edges_kernel,
        in_specs=[vmem] * 2,
        out_specs=[vmem] * 2,
        out_shape=[out, out],
        scratch_shapes=[pltpu.VMEM((4, count // LANES, width // 128, LANES * rows, 128), f32)],
        compiler_params=pltpu.CompilerParams(vmem_limit_bytes=16 * MIB),
        name="edges",
    )(vectors, spin_lines)


KEPT = REACH + 2
GROUP = 8


def inner_kernel(coef_ref, v_ref, s_ref, f_ref, kept_ref, there_ref, back_ref, rows_ref, r_ref, sp_ref, a_ref, b_ref, sum_ref, acc_ref):
    _, count, rows, width = v_ref.shape
    tiles = width // 128
    rho = ratios(coef_ref)

    there_ref[...] = shuffle(width)
    acc_ref[...] = jnp.zeros_like(acc_ref)
    for ref in (r_ref, a_ref, b_ref):
        ref[rows] = jnp.zeros(ref.shape[1:], jnp.float32)
    spins = s_ref[...].reshape(3 * rows, width) * -(coupling / hopping)
    for t, got in enumerate(moved_exactly(spins, there_ref[...])):
        for y in range(rows):
            for k in range(3):
                row = got[k * rows + y : k * rows + y + 1]
                sp_ref[y, k, :, t * 128 : (t + 1) * 128] = jnp.broadcast_to(row, (LANES, 128))

    def pass_over(dst, src, ratio, own=False):
        sum_ref[...] = src[0]

        @pl.loop(0, rows, step=GROUP)
        def _(start):
            below = [[sum_ref[k, :, t * 128 : (t + 1) * 128] for t in range(tiles)] for k in range(4)]
            for y in [start + i for i in range(GROUP)]:
                here = by_tile((src, (y,)))
                pairs = []
                for k in range(4):
                    right = on_right([x[k] for x in here])
                    pairs.append([right[t] + src[y + 1, k, :, t * 128 : (t + 1) * 128] for t in range(tiles)])
                left = [on_left(x) for x in below]
                for t in range(tiles):
                    x = plus([x[t] for x in pairs], [x[t] for x in left])
                    x = plus(x, on_site(here[t], load(sp_ref, (y,), t), ratio if own else None))
                    if not own:
                        x = plus(x, times(ratio, load(r_ref, (y,), t)))
                    dst(y, t, x)
                below = pairs
            for k in range(4):
                for t in range(tiles):
                    sum_ref[k, :, t * 128 : (t + 1) * 128] = below[k][t]

    def into(ref):
        return lambda y, t, x: save(ref, (y,), t, x)

    def fields(y, t, w):
        save(acc_ref, (y,), t, plus(density(load(r_ref, (y,), t), w), load(acc_ref, (y,), t)))

    @pl.loop(0, count // LANES)
    def _(g):
        states = v_ref[:, pl.ds(pl.multiple_of(g * LANES, LANES), LANES)]
        for t, got in enumerate(moved(states.reshape(4 * LANES * rows, width), there_ref[...])):
            rows_ref[t] = got

        for y in range(rows):
            for comp in range(4):
                for t in range(tiles):
                    at = pl.ds(comp * LANES * rows + y, LANES, stride=rows)
                    r_ref[y, comp, :, t * 128 : (t + 1) * 128] = rows_ref[t, at, :]

        pass_over(into(a_ref), r_ref, rho[3], own=True)
        pass_over(into(b_ref), a_ref, rho[2])
        for e in range(2):
            for i in range(REACH):
                kept_ref[g, e, i] = r_ref[rows - 1 - i if e else i]
            kept_ref[g, e, REACH] = a_ref[rows - 1 if e else 0]
            kept_ref[g, e, REACH + 1] = b_ref[rows - 1 if e else 0]
        pass_over(into(a_ref), b_ref, rho[1])
        pass_over(fields, a_ref, rho[0])

    for k in range(3):
        for y in range(0, rows, 8):
            for t in range(tiles):
                at = pl.ds(t * 128, 128)
                f_ref[k, y : y + 8, at] = side_by_side([acc_ref[y + i, k, :, at] for i in range(8)])
    back_ref[...] = shuffle(width, back=True)


def inner(coefficients, vectors, spins):
    _, count, rows, width = vectors.shape
    f32 = jnp.float32
    block = block_of(width)
    matrix = jax.ShapeDtypeStruct((block, block), jnp.bfloat16)
    state = pltpu.VMEM((rows + 1, 4, LANES, width), f32)
    vmem = pl.BlockSpec(memory_space=pltpu.VMEM)
    return pl.pallas_call(
        inner_kernel,
        in_specs=[pl.BlockSpec(memory_space=pltpu.SMEM), vmem, vmem],
        out_specs=[vmem] * 4,
        out_shape=[
            jax.ShapeDtypeStruct((3, rows, width), f32),
            jax.ShapeDtypeStruct((count // LANES, 2, KEPT, 4, LANES, width), f32),
            matrix,
            matrix,
        ],
        scratch_shapes=[
            pltpu.VMEM((width // 128, 4 * LANES * rows, 128), f32),
            state,
            pltpu.VMEM((rows, 3, LANES, width), f32),
            state,
            state,
            pltpu.VMEM((4, LANES, width), f32),
            pltpu.VMEM((rows, 3, LANES, width), f32),
        ],
        compiler_params=pltpu.CompilerParams(vmem_limit_bytes=40 * MIB),
        cost_estimate=pl.CostEstimate(flops=240 * vectors.size, bytes_accessed=8 * MIB, transcendentals=0),
        name="inner",
    )(coefficients, vectors, spins)


SPINS = ("B2", "B1", "A1", "A2", "A3", "B1 to A3")


def prepare(kept_ref, low_ref, high_ref, s_ref, there_ref, sp_ref, halo_ref, g_refs, ratio):
    _, rows, width = s_ref.shape
    parts = kept_ref.shape[0]
    tiles = width // 128
    end = HALO * 4 * parts * LANES
    matrix = there_ref[...]
    lines = []
    for e, ref in enumerate((low_ref, high_ref)):
        for k in range(3):
            at = end + k * HALO
            lines += [ref[at + i : at + i + 1] for i in ((1, 0) if e else (0, 1))]
            lines += [s_ref[k, y : y + 1] for y in ([rows - 1, rows - 2, rows - 3] if e else [0, 1, 2])]
    lines = jnp.concatenate(lines + lines[:2], axis=0) * -(coupling / hopping)
    for t, got in enumerate(moved_exactly(lines, matrix)):
        at = pl.ds(t * 128, 128)
        for e in range(2):
            for k in range(3):
                five = [got[(e * 3 + k) * 5 + i : (e * 3 + k) * 5 + i + 1] for i in range(5)]
                for i, row in enumerate(five + [five[1] + five[2] + five[3] + five[4]]):
                    sp_ref[e, i, k, :, at] = jnp.broadcast_to(row, (LANES, 128))
    for e, ref in enumerate((low_ref, high_ref)):
        for t, got in enumerate(moved(ref[:end].astype(jnp.bfloat16), matrix)):
            got = got.reshape(HALO, 4, parts, LANES, 128)
            for g in range(parts):
                halo_ref[g, e, :, :, :, t * 128 : (t + 1) * 128] = got[:, :, g]

    for e, ref in enumerate(g_refs):
        sums = [None] * tiles
        for g in range(parts):
            own = lambda i: (kept_ref, (g, e, i - 1))
            b1, b2 = (halo_ref, (g, e, 0)), (halo_ref, (g, e, 1))
            a3 = by_tile(own(3))
            sides = [beside([x[k] for x in a3]) for k in range(4)]
            for t in range(tiles):
                w = on_site(a3[t], load(sp_ref, (e, SPINS.index("B1 to A3")), t), ratio)
                w = plus(w, times(4.0, [x[t] for x in sides]), load(*own(4), t))
                here = density(load(*b1, t), w) + density(load(*b2, t), a3[t])
                sums[t] = here if g == 0 else plus(sums[t], here)
        for t, x in enumerate(sums):
            rows_out = [x[i * 3 + k] for k in range(3) for i in (range(HALO) if e else reversed(range(HALO)))]
            ref[:, t * 128 : (t + 1) * 128] = side_by_side(rows_out + rows_out[:2])


def cross(part, kept_ref, sp_ref, halo_ref, mid_ref, acc_ref, old_ref, rho):
    tiles = halo_ref.shape[-1] // 128

    @pl.loop(0, 2)
    def _(e):
        spin = lambda name: (sp_ref, (e, SPINS.index(name)))
        own = lambda i: (kept_ref, (part, e, i - 1))
        a_in, b_in = (kept_ref, (part, e, REACH)), (kept_ref, (part, e, REACH + 1))
        b1, b2 = (halo_ref, (part, e, 0)), (halo_ref, (part, e, 1))
        names = ("a_b2", "a_b1", "b_b2", "b_b1", "b_a1", "c_b1", "c_a1", "c_a2")
        mid = {name: (mid_ref, (i,)) for i, name in enumerate(names)}

        def make(row, at, others, ratio=None, extra=None):
            for t, x in flat(by_tile(row), spin(at), ratio):
                for ref, place in others:
                    x = plus(x, load(ref, place, t))
                if extra is not None:
                    x = plus(x, times(extra[0], load(*extra[1], t)))
                yield t, x

        def state(name, *rest, **more):
            for t, x in make(*rest, **more):
                save(*mid[name], t, x)

        def fields(i, r, w):
            for t, x in w:
                x = density(load(*r, t), x)
                if old_ref is not None:
                    x = plus(x, load(old_ref, (e, i), t))
                save(acc_ref, (e, i), t, x)

        state("a_b2", b2, "B2", [b1], ratio=rho[3])
        state("a_b1", b1, "B1", [b2, own(1)], ratio=rho[3])
        state("b_b2", mid["a_b2"], "B2", [mid["a_b1"], b2], extra=(rho[2], b2))
        state("b_b1", mid["a_b1"], "B1", [mid["a_b2"], a_in, b1], extra=(rho[2], b1))
        state("b_a1", b1, "A1", [mid["a_b1"]])
        state("c_b1", mid["b_b1"], "B1", [mid["b_b2"], b_in, mid["b_a1"]], extra=(rho[1], b1))
        state("c_a1", mid["b_a1"], "A1", [mid["b_b1"], b1])
        state("c_a2", b1, "A2", [mid["b_a1"]])
        fields(0, own(1), make(mid["c_a1"], "A1", [mid["c_b1"], mid["c_a2"]]))
        fields(1, own(2), make(mid["c_a2"], "A2", [mid["c_a1"], b1]))
        fields(2, own(3), make(b1, "A3", [mid["c_a2"]]))
        fields(3, own(4), ((t, load(*b1, t)) for t in range(tiles)))


def begin_kernel(coef_ref, kept_ref, low_ref, high_ref, s_ref, there_ref, sp_ref, halo_ref, g_low_ref, g_high_ref, acc_ref, mid_ref):
    rho = ratios(coef_ref)
    prepare(kept_ref, low_ref, high_ref, s_ref, there_ref, sp_ref, halo_ref, (g_low_ref, g_high_ref), rho[3])
    cross(0, kept_ref, sp_ref, halo_ref, mid_ref, acc_ref, None, rho)


def begin(coefficients, kept, low, high, spins, there):
    f32 = jnp.float32
    parts, width = kept.shape[0], spins.shape[-1]
    out = [
        (2, len(SPINS), 3, LANES, width),
        (parts, 2, HALO, 4, LANES, width),
        (8, width),
        (8, width),
        (2, REACH, 3, LANES, width),
    ]
    vmem = pl.BlockSpec(memory_space=pltpu.VMEM)
    return pl.pallas_call(
        begin_kernel,
        in_specs=[pl.BlockSpec(memory_space=pltpu.SMEM)] + [vmem] * 5,
        out_specs=[vmem] * len(out),
        out_shape=[jax.ShapeDtypeStruct(x, f32) for x in out],
        scratch_shapes=[pltpu.VMEM((8, 4, LANES, width), f32)],
        compiler_params=pltpu.CompilerParams(vmem_limit_bytes=32 * MIB),
        cost_estimate=pl.CostEstimate(flops=500 * low.size, bytes_accessed=4 * MIB, transcendentals=0),
        name="begin",
    )(coefficients, kept, low, high, spins, there)


def end_kernel(coef_ref, kept_ref, sp_ref, halo_ref, old_ref, f_ref, out_ref, mid_ref, acc_ref):
    _, rows, width = f_ref.shape
    parts = kept_ref.shape[0]
    rho = ratios(coef_ref)
    for part in range(1, parts):
        cross(part, kept_ref, sp_ref, halo_ref, mid_ref, acc_ref, old_ref if part == 1 else acc_ref, rho)
    last_ref = acc_ref if parts > 1 else old_ref
    out_ref[...] = f_ref[...]
    half = lax.broadcasted_iota(jnp.int32, (8, 128), 0) < REACH
    for t in range(width // 128):
        at = pl.ds(t * 128, 128)
        for k in range(3):
            low = [last_ref[0, i, k, :, at] for i in range(REACH)]
            high = [last_ref[1, i, k, :, at] for i in reversed(range(REACH))]
            edge = side_by_side(low + high)
            out_ref[k, :8, at] += jnp.where(half, edge, 0.0)
            out_ref[k, rows - 8 :, at] += jnp.where(half, 0.0, edge)


def end(coefficients, kept, sp, halo, old, f):
    f32 = jnp.float32
    vmem = pl.BlockSpec(memory_space=pltpu.VMEM)
    return pl.pallas_call(
        end_kernel,
        in_specs=[pl.BlockSpec(memory_space=pltpu.SMEM)] + [vmem] * 5,
        out_specs=vmem,
        out_shape=jax.ShapeDtypeStruct(f.shape, f32),
        scratch_shapes=[pltpu.VMEM((8, 4, LANES, f.shape[-1]), f32), pltpu.VMEM(old.shape, f32)],
        compiler_params=pltpu.CompilerParams(vmem_limit_bytes=32 * MIB),
        cost_estimate=pl.CostEstimate(flops=300 * kept.size, bytes_accessed=3 * MIB, transcendentals=0),
        name="end",
    )(coefficients, kept, sp, halo, old, f)


def sine_and_cosine(x):
    quarters = jnp.floor(x * (2.0 / jnp.pi) + 0.5)
    for part in (1.5703125, 4.837512969970703125e-4, 7.54978995489188216e-8):
        x = x - quarters * part
    z = x * x
    sine = ((-1.9515295891e-4 * z + 8.3321608736e-3) * z - 1.6666654611e-1) * z * x + x
    cosine = ((2.443315711809948e-5 * z - 1.388731625493765e-3) * z + 4.166664568298827e-2) * z * z - 0.5 * z + 1.0
    turns = quarters.astype(jnp.int32)
    odd, half = (turns & 1) == 1, (turns & 2) == 2
    sine, cosine = jnp.where(odd, cosine, sine), jnp.where(odd, -sine, cosine)
    return jnp.where(half, -sine, sine), jnp.where(half, -cosine, cosine)


def final_kernel(count_all, coef_ref, s_ref, back_ref, f_ref, other_ref, rotated_ref, fields_ref):
    _, rows, width = s_ref.shape
    total = f_ref[...] + other_ref[...]
    scale = ratios(coef_ref)[4][:1, :1] * (coupling / count_all)
    got = moved_exactly(total.reshape(3 * rows, width), back_ref[...])
    for t, x in enumerate(got):
        at = pl.ds(t * 128, 128)
        field = [x[k * rows : (k + 1) * rows] * scale for k in range(3)]
        spin = [s_ref[k, :, at] for k in range(3)]
        size = jnp.sqrt(field[0] * field[0] + field[1] * field[1] + field[2] * field[2])
        half_angle = (0.5 * time_step) * size
        sine, cosine = sine_and_cosine(half_angle)
        some = half_angle > 0.0
        ratio = jnp.where(some, sine / jnp.where(some, half_angle, 1.0), 1.0)
        along = field[0] * spin[0] + field[1] * spin[1] + field[2] * spin[2]
        keep = 1.0 - 2.0 * sine * sine
        turn = time_step * ratio * cosine
        lift = (0.5 * time_step * time_step) * ratio * ratio * along
        for k in range(3):
            i, j = (k + 1) % 3, (k + 2) % 3
            cross = field[i] * spin[j] - field[j] * spin[i]
            rotated_ref[k, :, at] = keep * spin[k] + turn * cross + lift * field[k]
            fields_ref[k, :, at] = field[k]


def final(coefficients, spins, back, count_all, f, other):
    out = jax.ShapeDtypeStruct(spins.shape, jnp.float32)
    vmem = pl.BlockSpec(memory_space=pltpu.VMEM)
    return pl.pallas_call(
        functools.partial(final_kernel, count_all),
        in_specs=[pl.BlockSpec(memory_space=pltpu.SMEM)] + [vmem] * 4,
        out_specs=[vmem] * 2,
        out_shape=[out, out],
        compiler_params=pltpu.CompilerParams(vmem_limit_bytes=32 * MIB),
        name="final",
    )(coefficients, spins, back, f, other)


def shards(vectors, classical_spins, coefficients):
    across, number = lax.axis_size("vec"), lax.axis_size("lat")
    count_all = vectors.shape[1] * across

    def to_row(x, on):
        return lax.ppermute(x, "lat", [(i, (i + on) % number) for i in range(number)])

    def swap(x, step):
        steps = across.bit_length() - 1
        bit = lambda i: 1 << (step if i % 2 == 0 else steps - 1 - step)
        pairs = [(i * across + j, i * across + (j ^ bit(i))) for i in range(number) for j in range(across)]
        return lax.ppermute(x, ("lat", "vec"), pairs)

    spins = classical_spins
    rows, width = spins.shape[1:]
    ends = jnp.stack([spins[:, :HALO], spins[:, rows - HALO :]]).reshape(2, 3 * HALO, width)
    low, high = edges(vectors, jnp.pad(ends, ((0, 0), (0, 8 - 3 * HALO), (0, 0))))
    from_below, from_above = to_row(high, 1), to_row(low, -1)
    f, kept, there, back = inner(coefficients, vectors, spins)
    sp, halo, g_low, g_high, crossed = begin(coefficients, kept, from_below, from_above, spins, there)
    below, above = to_row(g_high, 1), to_row(g_low, -1)
    fields = end(coefficients, kept, sp, halo, crossed, f)
    lines = lambda x: x[: 3 * HALO].reshape(3, HALO, width)
    fields = fields.at[:, :HALO].add(lines(below)).at[:, rows - HALO :].add(lines(above))
    steps = across.bit_length() - 1
    if across != 1 << steps or steps == 0:
        return final(coefficients, spins, back, count_all, lax.psum(fields, "vec"), jnp.zeros_like(fields))
    for step in range(steps - 1):
        fields = fields + swap(fields, step)
    return final(coefficients, spins, back, count_all, fields, swap(fields, steps - 1))


def solution(mesh):
    placed = (P(None, "vec", "lat", None), P(None, "lat", None), P())
    return jax.shard_map(
        shards,
        mesh=mesh,
        in_specs=placed,
        out_specs=(P(None, "lat", None), P(None, "lat", None)),
        check_vma=False,
    )
```

```python
import functools

import jax
import jax.numpy as jnp
from jax import lax
from jax.experimental import pallas as pl
from jax.experimental.pallas import tpu as pltpu
from jax.sharding import PartitionSpec as P

coupling = 2.0
hopping = 1.0
inverse_bound = 1.0 / 6.5
time_step = 1.0

LANES = 8
REACH = 4
HALO = 2
MIB = 1 << 20


def ratios(coefs):
    step = -hopping * inverse_bound
    c = [jnp.full((LANES, 128), coefs[k], jnp.float32) for k in range(5)]
    top = c[4] * (8.0 * step**4)
    under = 1.0 / top
    return [
        (c[0] - c[2] + c[4]) * under,
        (c[1] - 3.0 * c[3]) * step * under,
        (2.0 * c[2] - 8.0 * c[4]) * step**2 * under,
        4.0 * c[3] * step**3 * under,
        top,
    ]


def block_of(width):
    return next(b for b in (512, 256, 128) if width % b == 0)


def shuffle(width, back=False):
    block = block_of(width)
    tiles = block // 128
    source = lax.broadcasted_iota(jnp.int32, (block, block), 1 if back else 0)
    target = lax.broadcasted_iota(jnp.int32, (block, block), 0 if back else 1)
    place = lax.rem(source, tiles) * 128 + lax.div(source, tiles)
    return (place == target).astype(jnp.float32).astype(jnp.bfloat16)


def moved(states, matrix):
    block = matrix.shape[0]
    out = []
    for at in range(0, states.shape[1], block):
        got = jnp.dot(states[:, at : at + block], matrix, preferred_element_type=jnp.float32)
        out += [got[:, t : t + 128] for t in range(0, block, 128)]
    return out


def moved_exactly(rows, matrix):
    parts = []
    for _ in range(3):
        parts.append(rows.astype(jnp.bfloat16))
        rows = rows - parts[-1].astype(jnp.float32)
    count = rows.shape[0]
    got = moved(jnp.concatenate(parts, axis=0), matrix)
    return [x[:count] + x[count : 2 * count] + x[2 * count :] for x in got]


def on_left(tiles):
    group = block_of(len(tiles) * 128) // 128
    lane = lax.broadcasted_iota(jnp.int32, tiles[0].shape, 1)
    ends = [pltpu.roll(x, 1, 1) for x in tiles[group - 1 :: group]]
    if len(ends) > 1:
        ends = [jnp.where(lane == 0, ends[b - 1], x) for b, x in enumerate(ends)]
    return [tiles[t - 1] if t % group else ends[t // group] for t in range(len(tiles))]


def on_right(tiles):
    group = block_of(len(tiles) * 128) // 128
    lane = lax.broadcasted_iota(jnp.int32, tiles[0].shape, 1)
    starts = [pltpu.roll(x, 127, 1) for x in tiles[::group]]
    if len(starts) > 1:
        starts = [jnp.where(lane == 127, starts[(b + 1) % len(starts)], x) for b, x in enumerate(starts)]
    return [tiles[t + 1] if (t + 1) % group else starts[t // group] for t in range(len(tiles))]


def beside(tiles):
    return [x + y for x, y in zip(on_left(tiles), on_right(tiles))]


def on_site(state, spins, ratio=None):
    sx, sy, sz = spins
    ur, ui, dr, di = state
    zp, zm = (sz, sz) if ratio is None else (sz + ratio, sz - ratio)
    return [
        zp * ur + sx * dr + sy * di,
        zp * ui + sx * di - sy * dr,
        sx * ur - sy * ui - zm * dr,
        sx * ui + sy * ur - zm * di,
    ]


def density(r, w):
    return [
        r[0] * w[2] + r[1] * w[3] + r[2] * w[0] + r[3] * w[1],
        r[0] * w[3] - r[1] * w[2] - r[2] * w[1] + r[3] * w[0],
        r[0] * w[0] + r[1] * w[1] - r[2] * w[2] - r[3] * w[3],
    ]


def plus(*states):
    return [functools.reduce(lambda a, b: a + b, parts) for parts in zip(*states)]


def times(ratio, state):
    return [ratio * x for x in state]


def load(ref, at, t):
    return [ref[(*at, k, slice(None), pl.ds(t * 128, 128))] for k in range(ref.shape[len(at)])]


def save(ref, at, t, state):
    for k, x in enumerate(state):
        ref[(*at, k, slice(None), pl.ds(t * 128, 128))] = x


def by_tile(row):
    ref, at = row
    return [load(ref, at, t) for t in range(ref.shape[-1] // 128)]


def flat(row, spin, ratio=None):
    sides = [beside([x[k] for x in row]) for k in range(4)]
    for t, here in enumerate(row):
        yield t, plus([x[t] for x in sides], on_site(here, load(*spin, t), ratio))


def side_by_side(tiles):
    sub = lax.broadcasted_iota(jnp.int32, tiles[0].shape, 0)
    apart = 4
    while apart:
        first = (sub & apart) == 0
        tiles = [
            jnp.where(first, x + pltpu.roll(x, 8 - apart, 0), y + pltpu.roll(y, apart, 0))
            for x, y in zip(tiles[: len(tiles) // 2], tiles[len(tiles) // 2 :])
        ]
        apart //= 2
    return tiles[0]


def edges_kernel(v_ref, s_hbm, low_ref, high_ref, s_ref, rows_ref, s_sem):
    _, count, rows, width = v_ref.shape
    spins = pltpu.make_async_copy(s_hbm, s_ref, s_sem)
    spins.start()
    for comp in range(4):
        for g in range(count // LANES):
            states = v_ref[comp, g * LANES : (g + 1) * LANES].astype(jnp.float32).reshape(LANES * rows, width)
            for t in range(width // 128):
                rows_ref[comp, g, t] = states[:, t * 128 : (t + 1) * 128]
            for i in range(HALO):
                to = pl.ds((i * 4 + comp) * count + g * LANES, LANES)
                for t in range(width // 128):
                    at = pl.ds(t * 128, 128)
                    low_ref[to, at] = rows_ref[comp, g, t, pl.ds(i, LANES, stride=rows), :]
                    high_ref[to, at] = rows_ref[comp, g, t, pl.ds(rows - 1 - i, LANES, stride=rows), :]
    spins.wait()
    end = HALO * 4 * count
    for ref, first in ((low_ref, 0), (high_ref, rows - HALO)):
        lines = [s_ref[k, first + i : first + i + 1] for k in range(3) for i in range(HALO)]
        ref[end:] = jnp.concatenate(lines + lines[: 8 - 3 * HALO], axis=0)


def edges(vectors, spins):
    _, count, rows, width = vectors.shape
    f32 = jnp.float32
    out = pltpu.VMEM((HALO * 4 * count + 8, width), f32)
    vmem = pl.BlockSpec(memory_space=pltpu.VMEM)
    return pl.pallas_call(
        edges_kernel,
        in_specs=[vmem, pl.BlockSpec(memory_space=pltpu.HBM)],
        out_specs=[vmem] * 3,
        out_shape=[out, out, pltpu.VMEM(spins.shape, f32)],
        scratch_shapes=[
            pltpu.VMEM((4, count // LANES, width // 128, LANES * rows, 128), f32),
            pltpu.SemaphoreType.DMA,
        ],
        compiler_params=pltpu.CompilerParams(vmem_limit_bytes=16 * MIB),
        name="edges",
    )(vectors, pltpu.with_memory_space_constraint(spins, pltpu.HBM))


KEPT = REACH + 2
GROUP = 8


def inner_kernel(coef_ref, v_ref, s_ref, f_ref, kept_ref, there_ref, back_ref, rows_ref, r_ref, sp_ref, a_ref, b_ref, sum_ref, acc_ref):
    _, count, rows, width = v_ref.shape
    tiles = width // 128
    rho = ratios(coef_ref)

    there_ref[...] = shuffle(width)
    acc_ref[...] = jnp.zeros_like(acc_ref)
    for ref in (r_ref, a_ref, b_ref):
        ref[rows] = jnp.zeros(ref.shape[1:], jnp.float32)
    spins = s_ref[...].reshape(3 * rows, width) * -(coupling / hopping)
    for t, got in enumerate(moved_exactly(spins, there_ref[...])):
        for y in range(rows):
            for k in range(3):
                row = got[k * rows + y : k * rows + y + 1]
                sp_ref[y, k, :, t * 128 : (t + 1) * 128] = jnp.broadcast_to(row, (LANES, 128))

    def pass_over(dst, src, ratio, own=False):
        sum_ref[...] = src[0]

        @pl.loop(0, rows, step=GROUP)
        def _(start):
            below = [[sum_ref[k, :, t * 128 : (t + 1) * 128] for t in range(tiles)] for k in range(4)]
            for y in [start + i for i in range(GROUP)]:
                here = by_tile((src, (y,)))
                pairs = []
                for k in range(4):
                    right = on_right([x[k] for x in here])
                    pairs.append([right[t] + src[y + 1, k, :, t * 128 : (t + 1) * 128] for t in range(tiles)])
                left = [on_left(x) for x in below]
                for t in range(tiles):
                    x = plus([x[t] for x in pairs], [x[t] for x in left])
                    x = plus(x, on_site(here[t], load(sp_ref, (y,), t), ratio if own else None))
                    if not own:
                        x = plus(x, times(ratio, load(r_ref, (y,), t)))
                    dst(y, t, x)
                below = pairs
            for k in range(4):
                for t in range(tiles):
                    sum_ref[k, :, t * 128 : (t + 1) * 128] = below[k][t]

    def into(ref):
        return lambda y, t, x: save(ref, (y,), t, x)

    def fields(y, t, w):
        save(acc_ref, (y,), t, plus(density(load(r_ref, (y,), t), w), load(acc_ref, (y,), t)))

    @pl.loop(0, count // LANES)
    def _(g):
        states = v_ref[:, pl.ds(pl.multiple_of(g * LANES, LANES), LANES)]
        for t, got in enumerate(moved(states.reshape(4 * LANES * rows, width), there_ref[...])):
            rows_ref[t] = got

        for y in range(rows):
            for comp in range(4):
                for t in range(tiles):
                    at = pl.ds(comp * LANES * rows + y, LANES, stride=rows)
                    r_ref[y, comp, :, t * 128 : (t + 1) * 128] = rows_ref[t, at, :]

        pass_over(into(a_ref), r_ref, rho[3], own=True)
        pass_over(into(b_ref), a_ref, rho[2])
        for e in range(2):
            for i in range(REACH):
                kept_ref[g, e, i] = r_ref[rows - 1 - i if e else i]
            kept_ref[g, e, REACH] = a_ref[rows - 1 if e else 0]
            kept_ref[g, e, REACH + 1] = b_ref[rows - 1 if e else 0]
        pass_over(into(a_ref), b_ref, rho[1])
        pass_over(fields, a_ref, rho[0])

    for k in range(3):
        for y in range(0, rows, 8):
            for t in range(tiles):
                at = pl.ds(t * 128, 128)
                f_ref[k, y : y + 8, at] = side_by_side([acc_ref[y + i, k, :, at] for i in range(8)])
    back_ref[...] = shuffle(width, back=True)


def inner(coefficients, vectors, spins):
    _, count, rows, width = vectors.shape
    f32 = jnp.float32
    block = block_of(width)
    matrix = jax.ShapeDtypeStruct((block, block), jnp.bfloat16)
    state = pltpu.VMEM((rows + 1, 4, LANES, width), f32)
    vmem = pl.BlockSpec(memory_space=pltpu.VMEM)
    return pl.pallas_call(
        inner_kernel,
        in_specs=[pl.BlockSpec(memory_space=pltpu.SMEM), vmem, vmem],
        out_specs=[vmem] * 4,
        out_shape=[
            jax.ShapeDtypeStruct((3, rows, width), f32),
            jax.ShapeDtypeStruct((count // LANES, 2, KEPT, 4, LANES, width), f32),
            matrix,
            matrix,
        ],
        scratch_shapes=[
            pltpu.VMEM((width // 128, 4 * LANES * rows, 128), f32),
            state,
            pltpu.VMEM((rows, 3, LANES, width), f32),
            state,
            state,
            pltpu.VMEM((4, LANES, width), f32),
            pltpu.VMEM((rows, 3, LANES, width), f32),
        ],
        compiler_params=pltpu.CompilerParams(vmem_limit_bytes=40 * MIB),
        cost_estimate=pl.CostEstimate(flops=240 * vectors.size, bytes_accessed=8 * MIB, transcendentals=0),
        name="inner",
    )(coefficients, vectors, spins)


SPINS = ("B2", "B1", "A1", "A2", "A3", "B1 to A3")


def prepare(kept_ref, low_ref, high_ref, s_ref, there_ref, sp_ref, halo_ref, g_refs, ratio):
    _, rows, width = s_ref.shape
    parts = kept_ref.shape[0]
    tiles = width // 128
    end = HALO * 4 * parts * LANES
    matrix = there_ref[...]
    lines = []
    for e, ref in enumerate((low_ref, high_ref)):
        for k in range(3):
            at = end + k * HALO
            lines += [ref[at + i : at + i + 1] for i in ((1, 0) if e else (0, 1))]
            lines += [s_ref[k, y : y + 1] for y in ([rows - 1, rows - 2, rows - 3] if e else [0, 1, 2])]
    lines = jnp.concatenate(lines + lines[:2], axis=0) * -(coupling / hopping)
    for t, got in enumerate(moved_exactly(lines, matrix)):
        at = pl.ds(t * 128, 128)
        for e in range(2):
            for k in range(3):
                five = [got[(e * 3 + k) * 5 + i : (e * 3 + k) * 5 + i + 1] for i in range(5)]
                for i, row in enumerate(five + [five[1] + five[2] + five[3] + five[4]]):
                    sp_ref[e, i, k, :, at] = jnp.broadcast_to(row, (LANES, 128))
    for e, ref in enumerate((low_ref, high_ref)):
        for t, got in enumerate(moved(ref[:end].astype(jnp.bfloat16), matrix)):
            got = got.reshape(HALO, 4, parts, LANES, 128)
            for g in range(parts):
                halo_ref[g, e, :, :, :, t * 128 : (t + 1) * 128] = got[:, :, g]

    for e, ref in enumerate(g_refs):
        sums = [None] * tiles
        for g in range(parts):
            own = lambda i: (kept_ref, (g, e, i - 1))
            b1, b2 = (halo_ref, (g, e, 0)), (halo_ref, (g, e, 1))
            a3 = by_tile(own(3))
            sides = [beside([x[k] for x in a3]) for k in range(4)]
            for t in range(tiles):
                w = on_site(a3[t], load(sp_ref, (e, SPINS.index("B1 to A3")), t), ratio)
                w = plus(w, times(4.0, [x[t] for x in sides]), load(*own(4), t))
                here = density(load(*b1, t), w) + density(load(*b2, t), a3[t])
                sums[t] = here if g == 0 else plus(sums[t], here)
        for t, x in enumerate(sums):
            rows_out = [x[i * 3 + k] for k in range(3) for i in (range(HALO) if e else reversed(range(HALO)))]
            ref[:, t * 128 : (t + 1) * 128] = side_by_side(rows_out + rows_out[:2])


def cross(part, kept_ref, sp_ref, halo_ref, mid_ref, acc_ref, old_ref, rho):
    tiles = halo_ref.shape[-1] // 128

    @pl.loop(0, 2)
    def _(e):
        spin = lambda name: (sp_ref, (e, SPINS.index(name)))
        own = lambda i: (kept_ref, (part, e, i - 1))
        a_in, b_in = (kept_ref, (part, e, REACH)), (kept_ref, (part, e, REACH + 1))
        b1, b2 = (halo_ref, (part, e, 0)), (halo_ref, (part, e, 1))
        names = ("a_b2", "a_b1", "b_b2", "b_b1", "b_a1", "c_b1", "c_a1", "c_a2")
        mid = {name: (mid_ref, (i,)) for i, name in enumerate(names)}

        def make(row, at, others, ratio=None, extra=None):
            for t, x in flat(by_tile(row), spin(at), ratio):
                for ref, place in others:
                    x = plus(x, load(ref, place, t))
                if extra is not None:
                    x = plus(x, times(extra[0], load(*extra[1], t)))
                yield t, x

        def state(name, *rest, **more):
            for t, x in make(*rest, **more):
                save(*mid[name], t, x)

        def fields(i, r, w):
            for t, x in w:
                x = density(load(*r, t), x)
                if old_ref is not None:
                    x = plus(x, load(old_ref, (e, i), t))
                save(acc_ref, (e, i), t, x)

        state("a_b2", b2, "B2", [b1], ratio=rho[3])
        state("a_b1", b1, "B1", [b2, own(1)], ratio=rho[3])
        state("b_b2", mid["a_b2"], "B2", [mid["a_b1"], b2], extra=(rho[2], b2))
        state("b_b1", mid["a_b1"], "B1", [mid["a_b2"], a_in, b1], extra=(rho[2], b1))
        state("b_a1", b1, "A1", [mid["a_b1"]])
        state("c_b1", mid["b_b1"], "B1", [mid["b_b2"], b_in, mid["b_a1"]], extra=(rho[1], b1))
        state("c_a1", mid["b_a1"], "A1", [mid["b_b1"], b1])
        state("c_a2", b1, "A2", [mid["b_a1"]])
        fields(0, own(1), make(mid["c_a1"], "A1", [mid["c_b1"], mid["c_a2"]]))
        fields(1, own(2), make(mid["c_a2"], "A2", [mid["c_a1"], b1]))
        fields(2, own(3), make(b1, "A3", [mid["c_a2"]]))
        fields(3, own(4), ((t, load(*b1, t)) for t in range(tiles)))


def begin_kernel(coef_ref, kept_ref, low_ref, high_ref, s_ref, there_ref, sp_ref, halo_ref, g_low_ref, g_high_ref, acc_ref, mid_ref):
    rho = ratios(coef_ref)
    prepare(kept_ref, low_ref, high_ref, s_ref, there_ref, sp_ref, halo_ref, (g_low_ref, g_high_ref), rho[3])
    cross(0, kept_ref, sp_ref, halo_ref, mid_ref, acc_ref, None, rho)


def begin(coefficients, kept, low, high, spins, there):
    f32 = jnp.float32
    parts, width = kept.shape[0], spins.shape[-1]
    out = [
        (2, len(SPINS), 3, LANES, width),
        (parts, 2, HALO, 4, LANES, width),
        (8, width),
        (8, width),
        (2, REACH, 3, LANES, width),
    ]
    vmem = pl.BlockSpec(memory_space=pltpu.VMEM)
    return pl.pallas_call(
        begin_kernel,
        in_specs=[pl.BlockSpec(memory_space=pltpu.SMEM)] + [vmem] * 5,
        out_specs=[vmem] * len(out),
        out_shape=[jax.ShapeDtypeStruct(x, f32) for x in out],
        scratch_shapes=[pltpu.VMEM((8, 4, LANES, width), f32)],
        compiler_params=pltpu.CompilerParams(vmem_limit_bytes=32 * MIB),
        cost_estimate=pl.CostEstimate(flops=500 * low.size, bytes_accessed=4 * MIB, transcendentals=0),
        name="begin",
    )(coefficients, kept, low, high, spins, there)


def end_kernel(coef_ref, kept_ref, sp_ref, halo_ref, old_ref, f_ref, out_ref, mid_ref, acc_ref):
    _, rows, width = f_ref.shape
    parts = kept_ref.shape[0]
    rho = ratios(coef_ref)
    for part in range(1, parts):
        cross(part, kept_ref, sp_ref, halo_ref, mid_ref, acc_ref, old_ref if part == 1 else acc_ref, rho)
    last_ref = acc_ref if parts > 1 else old_ref
    out_ref[...] = f_ref[...]
    half = lax.broadcasted_iota(jnp.int32, (8, 128), 0) < REACH
    for t in range(width // 128):
        at = pl.ds(t * 128, 128)
        for k in range(3):
            low = [last_ref[0, i, k, :, at] for i in range(REACH)]
            high = [last_ref[1, i, k, :, at] for i in reversed(range(REACH))]
            edge = side_by_side(low + high)
            out_ref[k, :8, at] += jnp.where(half, edge, 0.0)
            out_ref[k, rows - 8 :, at] += jnp.where(half, 0.0, edge)


def end(coefficients, kept, sp, halo, old, f):
    f32 = jnp.float32
    vmem = pl.BlockSpec(memory_space=pltpu.VMEM)
    return pl.pallas_call(
        end_kernel,
        in_specs=[pl.BlockSpec(memory_space=pltpu.SMEM)] + [vmem] * 5,
        out_specs=vmem,
        out_shape=jax.ShapeDtypeStruct(f.shape, f32),
        scratch_shapes=[pltpu.VMEM((8, 4, LANES, f.shape[-1]), f32), pltpu.VMEM(old.shape, f32)],
        compiler_params=pltpu.CompilerParams(vmem_limit_bytes=32 * MIB),
        cost_estimate=pl.CostEstimate(flops=300 * kept.size, bytes_accessed=3 * MIB, transcendentals=0),
        name="end",
    )(coefficients, kept, sp, halo, old, f)


def sine_and_cosine(x):
    quarters = jnp.floor(x * (2.0 / jnp.pi) + 0.5)
    for part in (1.5703125, 4.837512969970703125e-4, 7.54978995489188216e-8):
        x = x - quarters * part
    z = x * x
    sine = ((-1.9515295891e-4 * z + 8.3321608736e-3) * z - 1.6666654611e-1) * z * x + x
    cosine = ((2.443315711809948e-5 * z - 1.388731625493765e-3) * z + 4.166664568298827e-2) * z * z - 0.5 * z + 1.0
    turns = quarters.astype(jnp.int32)
    odd, half = (turns & 1) == 1, (turns & 2) == 2
    sine, cosine = jnp.where(odd, cosine, sine), jnp.where(odd, -sine, cosine)
    return jnp.where(half, -sine, sine), jnp.where(half, -cosine, cosine)


def final_kernel(count_all, coef_ref, s_ref, back_ref, f_ref, other_ref, rotated_ref, fields_ref):
    _, rows, width = s_ref.shape
    total = f_ref[...] + other_ref[...]
    scale = ratios(coef_ref)[4][:1, :1] * (coupling / count_all)
    got = moved_exactly(total.reshape(3 * rows, width), back_ref[...])
    for t, x in enumerate(got):
        at = pl.ds(t * 128, 128)
        field = [x[k * rows : (k + 1) * rows] * scale for k in range(3)]
        spin = [s_ref[k, :, at] for k in range(3)]
        size = jnp.sqrt(field[0] * field[0] + field[1] * field[1] + field[2] * field[2])
        half_angle = (0.5 * time_step) * size
        sine, cosine = sine_and_cosine(half_angle)
        some = half_angle > 0.0
        ratio = jnp.where(some, sine / jnp.where(some, half_angle, 1.0), 1.0)
        along = field[0] * spin[0] + field[1] * spin[1] + field[2] * spin[2]
        keep = 1.0 - 2.0 * sine * sine
        turn = time_step * ratio * cosine
        lift = (0.5 * time_step * time_step) * ratio * ratio * along
        for k in range(3):
            i, j = (k + 1) % 3, (k + 2) % 3
            cross = field[i] * spin[j] - field[j] * spin[i]
            rotated_ref[k, :, at] = keep * spin[k] + turn * cross + lift * field[k]
            fields_ref[k, :, at] = field[k]


def final(coefficients, spins, back, count_all, f, other):
    out = jax.ShapeDtypeStruct(spins.shape, jnp.float32)
    vmem = pl.BlockSpec(memory_space=pltpu.VMEM)
    return pl.pallas_call(
        functools.partial(final_kernel, count_all),
        in_specs=[pl.BlockSpec(memory_space=pltpu.SMEM)] + [vmem] * 4,
        out_specs=[vmem] * 2,
        out_shape=[out, out],
        compiler_params=pltpu.CompilerParams(vmem_limit_bytes=32 * MIB),
        name="final",
    )(coefficients, spins, back, f, other)


def shards(vectors, classical_spins, coefficients):
    across, number = lax.axis_size("vec"), lax.axis_size("lat")
    count_all = vectors.shape[1] * across

    def to_row(x, on):
        return lax.ppermute(x, "lat", [(i, (i + on) % number) for i in range(number)])

    def swap(x, step):
        steps = across.bit_length() - 1
        bit = lambda i: 1 << (step if i % 2 == 0 else steps - 1 - step)
        pairs = [(i * across + j, i * across + (j ^ bit(i))) for i in range(number) for j in range(across)]
        return lax.ppermute(x, ("lat", "vec"), pairs)

    rows, width = classical_spins.shape[1:]
    low, high, spins = edges(vectors, classical_spins)
    from_below, from_above = to_row(high, 1), to_row(low, -1)
    f, kept, there, back = inner(coefficients, vectors, spins)
    sp, halo, g_low, g_high, crossed = begin(coefficients, kept, from_below, from_above, spins, there)
    below, above = to_row(g_high, 1), to_row(g_low, -1)
    fields = end(coefficients, kept, sp, halo, crossed, f)
    lines = lambda x: x[: 3 * HALO].reshape(3, HALO, width)
    fields = fields.at[:, :HALO].add(lines(below)).at[:, rows - HALO :].add(lines(above))
    steps = across.bit_length() - 1
    if across != 1 << steps or steps == 0:
        return final(coefficients, spins, back, count_all, lax.psum(fields, "vec"), jnp.zeros_like(fields))
    for step in range(steps - 1):
        fields = fields + swap(fields, step)
    return final(coefficients, spins, back, count_all, fields, swap(fields, steps - 1))


def solution(mesh):
    placed = (P(None, "vec", "lat", None), P(None, "lat", None), P())
    return jax.shard_map(
        shards,
        mesh=mesh,
        in_specs=placed,
        out_specs=(P(None, "lat", None), P(None, "lat", None)),
        check_vma=False,
    )
```

```python
import functools

import jax
import jax.numpy as jnp
from jax import lax
from jax.experimental import pallas as pl
from jax.experimental.pallas import tpu as pltpu
from jax.sharding import PartitionSpec as P

coupling = 2.0
hopping = 1.0
inverse_bound = 1.0 / 6.5
time_step = 1.0

LANES = 8
REACH = 4
HALO = 2
MIB = 1 << 20


def ratios(coefs):
    step = -hopping * inverse_bound
    c = [jnp.full((LANES, 128), coefs[k], jnp.float32) for k in range(5)]
    top = c[4] * (8.0 * step**4)
    under = 1.0 / top
    return [
        (c[0] - c[2] + c[4]) * under,
        (c[1] - 3.0 * c[3]) * step * under,
        (2.0 * c[2] - 8.0 * c[4]) * step**2 * under,
        4.0 * c[3] * step**3 * under,
        top,
    ]


def block_of(width):
    return next(b for b in (512, 256, 128) if width % b == 0)


def shuffle(width, back=False):
    block = block_of(width)
    tiles = block // 128
    source = lax.broadcasted_iota(jnp.int32, (block, block), 1 if back else 0)
    target = lax.broadcasted_iota(jnp.int32, (block, block), 0 if back else 1)
    place = lax.rem(source, tiles) * 128 + lax.div(source, tiles)
    return (place == target).astype(jnp.float32).astype(jnp.bfloat16)


def moved(states, matrix):
    block = matrix.shape[0]
    out = []
    for at in range(0, states.shape[1], block):
        got = jnp.dot(states[:, at : at + block], matrix, preferred_element_type=jnp.float32)
        out += [got[:, t : t + 128] for t in range(0, block, 128)]
    return out


def moved_exactly(rows, matrix):
    parts = []
    for _ in range(3):
        parts.append(rows.astype(jnp.bfloat16))
        rows = rows - parts[-1].astype(jnp.float32)
    count = rows.shape[0]
    got = moved(jnp.concatenate(parts, axis=0), matrix)
    return [x[:count] + x[count : 2 * count] + x[2 * count :] for x in got]


def on_left(tiles):
    group = block_of(len(tiles) * 128) // 128
    lane = lax.broadcasted_iota(jnp.int32, tiles[0].shape, 1)
    ends = [pltpu.roll(x, 1, 1) for x in tiles[group - 1 :: group]]
    if len(ends) > 1:
        ends = [jnp.where(lane == 0, ends[b - 1], x) for b, x in enumerate(ends)]
    return [tiles[t - 1] if t % group else ends[t // group] for t in range(len(tiles))]


def on_right(tiles):
    group = block_of(len(tiles) * 128) // 128
    lane = lax.broadcasted_iota(jnp.int32, tiles[0].shape, 1)
    starts = [pltpu.roll(x, 127, 1) for x in tiles[::group]]
    if len(starts) > 1:
        starts = [jnp.where(lane == 127, starts[(b + 1) % len(starts)], x) for b, x in enumerate(starts)]
    return [tiles[t + 1] if (t + 1) % group else starts[t // group] for t in range(len(tiles))]


def beside(tiles):
    return [x + y for x, y in zip(on_left(tiles), on_right(tiles))]


def on_site(state, spins, ratio=None):
    sx, sy, sz = spins
    ur, ui, dr, di = state
    zp, zm = (sz, sz) if ratio is None else (sz + ratio, sz - ratio)
    return [
        zp * ur + sx * dr + sy * di,
        zp * ui + sx * di - sy * dr,
        sx * ur - sy * ui - zm * dr,
        sx * ui + sy * ur - zm * di,
    ]


def density(r, w):
    return [
        r[0] * w[2] + r[1] * w[3] + r[2] * w[0] + r[3] * w[1],
        r[0] * w[3] - r[1] * w[2] - r[2] * w[1] + r[3] * w[0],
        r[0] * w[0] + r[1] * w[1] - r[2] * w[2] - r[3] * w[3],
    ]


def plus(*states):
    return [functools.reduce(lambda a, b: a + b, parts) for parts in zip(*states)]


def times(ratio, state):
    return [ratio * x for x in state]


def load(ref, at, t):
    return [ref[(*at, k, slice(None), pl.ds(t * 128, 128))] for k in range(ref.shape[len(at)])]


def save(ref, at, t, state):
    for k, x in enumerate(state):
        ref[(*at, k, slice(None), pl.ds(t * 128, 128))] = x


def by_tile(row):
    ref, at = row
    return [load(ref, at, t) for t in range(ref.shape[-1] // 128)]


def flat(row, spin, ratio=None):
    sides = [beside([x[k] for x in row]) for k in range(4)]
    for t, here in enumerate(row):
        yield t, plus([x[t] for x in sides], on_site(here, load(*spin, t), ratio))


def side_by_side(tiles):
    sub = lax.broadcasted_iota(jnp.int32, tiles[0].shape, 0)
    apart = 4
    while apart:
        first = (sub & apart) == 0
        tiles = [
            jnp.where(first, x + pltpu.roll(x, 8 - apart, 0), y + pltpu.roll(y, apart, 0))
            for x, y in zip(tiles[: len(tiles) // 2], tiles[len(tiles) // 2 :])
        ]
        apart //= 2
    return tiles[0]


def edges_kernel(v_hbm, s_hbm, low_ref, high_ref, v_ref, s_ref, rows_ref, v_sem, s_sem):
    _, count, rows, width = v_hbm.shape
    copies = [pltpu.make_async_copy(v_hbm.at[comp], v_ref.at[comp], v_sem.at[comp]) for comp in range(4)]
    for copy in copies:
        copy.start()
    spins = pltpu.make_async_copy(s_hbm, s_ref, s_sem)
    spins.start()
    for comp in range(4):
        copies[comp].wait()
        for g in range(count // LANES):
            states = v_ref[comp, g * LANES : (g + 1) * LANES].astype(jnp.float32).reshape(LANES * rows, width)
            for t in range(width // 128):
                rows_ref[comp, g, t] = states[:, t * 128 : (t + 1) * 128]
            for i in range(HALO):
                to = pl.ds((i * 4 + comp) * count + g * LANES, LANES)
                for t in range(width // 128):
                    at = pl.ds(t * 128, 128)
                    low_ref[to, at] = rows_ref[comp, g, t, pl.ds(i, LANES, stride=rows), :]
                    high_ref[to, at] = rows_ref[comp, g, t, pl.ds(rows - 1 - i, LANES, stride=rows), :]
    spins.wait()
    end = HALO * 4 * count
    for ref, first in ((low_ref, 0), (high_ref, rows - HALO)):
        lines = [s_ref[k, first + i : first + i + 1] for k in range(3) for i in range(HALO)]
        ref[end:] = jnp.concatenate(lines + lines[: 8 - 3 * HALO], axis=0)


def edges(vectors, spins):
    _, count, rows, width = vectors.shape
    f32 = jnp.float32
    out = pltpu.VMEM((HALO * 4 * count + 8, width), f32)
    hbm, vmem = pl.BlockSpec(memory_space=pltpu.HBM), pl.BlockSpec(memory_space=pltpu.VMEM)
    return pl.pallas_call(
        edges_kernel,
        in_specs=[hbm] * 2,
        out_specs=[vmem] * 4,
        out_shape=[out, out, pltpu.VMEM(vectors.shape, vectors.dtype), pltpu.VMEM(spins.shape, f32)],
        scratch_shapes=[
            pltpu.VMEM((4, count // LANES, width // 128, LANES * rows, 128), f32),
            pltpu.SemaphoreType.DMA((4,)),
            pltpu.SemaphoreType.DMA,
        ],
        compiler_params=pltpu.CompilerParams(vmem_limit_bytes=16 * MIB),
        name="edges",
    )(*[pltpu.with_memory_space_constraint(x, pltpu.HBM) for x in (vectors, spins)])


KEPT = REACH + 2
GROUP = 8


def inner_kernel(coef_ref, v_ref, s_ref, f_ref, kept_ref, there_ref, back_ref, rows_ref, r_ref, sp_ref, a_ref, b_ref, sum_ref, acc_ref):
    _, count, rows, width = v_ref.shape
    tiles = width // 128
    rho = ratios(coef_ref)

    there_ref[...] = shuffle(width)
    acc_ref[...] = jnp.zeros_like(acc_ref)
    for ref in (r_ref, a_ref, b_ref):
        ref[rows] = jnp.zeros(ref.shape[1:], jnp.float32)
    spins = s_ref[...].reshape(3 * rows, width) * -(coupling / hopping)
    for t, got in enumerate(moved_exactly(spins, there_ref[...])):
        for y in range(rows):
            for k in range(3):
                row = got[k * rows + y : k * rows + y + 1]
                sp_ref[y, k, :, t * 128 : (t + 1) * 128] = jnp.broadcast_to(row, (LANES, 128))

    def pass_over(dst, src, ratio, own=False):
        sum_ref[...] = src[0]

        @pl.loop(0, rows, step=GROUP)
        def _(start):
            below = [[sum_ref[k, :, t * 128 : (t + 1) * 128] for t in range(tiles)] for k in range(4)]
            for y in [start + i for i in range(GROUP)]:
                here = by_tile((src, (y,)))
                pairs = []
                for k in range(4):
                    right = on_right([x[k] for x in here])
                    pairs.append([right[t] + src[y + 1, k, :, t * 128 : (t + 1) * 128] for t in range(tiles)])
                left = [on_left(x) for x in below]
                for t in range(tiles):
                    x = plus([x[t] for x in pairs], [x[t] for x in left])
                    x = plus(x, on_site(here[t], load(sp_ref, (y,), t), ratio if own else None))
                    if not own:
                        x = plus(x, times(ratio, load(r_ref, (y,), t)))
                    dst(y, t, x)
                below = pairs
            for k in range(4):
                for t in range(tiles):
                    sum_ref[k, :, t * 128 : (t + 1) * 128] = below[k][t]

    def into(ref):
        return lambda y, t, x: save(ref, (y,), t, x)

    def fields(y, t, w):
        save(acc_ref, (y,), t, plus(density(load(r_ref, (y,), t), w), load(acc_ref, (y,), t)))

    @pl.loop(0, count // LANES)
    def _(g):
        states = v_ref[:, pl.ds(pl.multiple_of(g * LANES, LANES), LANES)]
        for t, got in enumerate(moved(states.reshape(4 * LANES * rows, width), there_ref[...])):
            rows_ref[t] = got

        for y in range(rows):
            for comp in range(4):
                for t in range(tiles):
                    at = pl.ds(comp * LANES * rows + y, LANES, stride=rows)
                    r_ref[y, comp, :, t * 128 : (t + 1) * 128] = rows_ref[t, at, :]

        pass_over(into(a_ref), r_ref, rho[3], own=True)
        pass_over(into(b_ref), a_ref, rho[2])
        for e in range(2):
            for i in range(REACH):
                kept_ref[g, e, i] = r_ref[rows - 1 - i if e else i]
            kept_ref[g, e, REACH] = a_ref[rows - 1 if e else 0]
            kept_ref[g, e, REACH + 1] = b_ref[rows - 1 if e else 0]
        pass_over(into(a_ref), b_ref, rho[1])
        pass_over(fields, a_ref, rho[0])

    for k in range(3):
        for y in range(0, rows, 8):
            for t in range(tiles):
                at = pl.ds(t * 128, 128)
                f_ref[k, y : y + 8, at] = side_by_side([acc_ref[y + i, k, :, at] for i in range(8)])
    back_ref[...] = shuffle(width, back=True)


def inner(coefficients, vectors, spins):
    _, count, rows, width = vectors.shape
    f32 = jnp.float32
    block = block_of(width)
    matrix = jax.ShapeDtypeStruct((block, block), jnp.bfloat16)
    state = pltpu.VMEM((rows + 1, 4, LANES, width), f32)
    vmem = pl.BlockSpec(memory_space=pltpu.VMEM)
    return pl.pallas_call(
        inner_kernel,
        in_specs=[pl.BlockSpec(memory_space=pltpu.SMEM), vmem, vmem],
        out_specs=[vmem] * 4,
        out_shape=[
            jax.ShapeDtypeStruct((3, rows, width), f32),
            jax.ShapeDtypeStruct((count // LANES, 2, KEPT, 4, LANES, width), f32),
            matrix,
            matrix,
        ],
        scratch_shapes=[
            pltpu.VMEM((width // 128, 4 * LANES * rows, 128), f32),
            state,
            pltpu.VMEM((rows, 3, LANES, width), f32),
            state,
            state,
            pltpu.VMEM((4, LANES, width), f32),
            pltpu.VMEM((rows, 3, LANES, width), f32),
        ],
        compiler_params=pltpu.CompilerParams(vmem_limit_bytes=40 * MIB),
        cost_estimate=pl.CostEstimate(flops=240 * vectors.size, bytes_accessed=8 * MIB, transcendentals=0),
        name="inner",
    )(coefficients, vectors, spins)


SPINS = ("B2", "B1", "A1", "A2", "A3", "B1 to A3")


def prepare(kept_ref, low_ref, high_ref, s_ref, there_ref, sp_ref, halo_ref, g_refs, ratio):
    _, rows, width = s_ref.shape
    parts = kept_ref.shape[0]
    tiles = width // 128
    end = HALO * 4 * parts * LANES
    matrix = there_ref[...]
    lines = []
    for e, ref in enumerate((low_ref, high_ref)):
        for k in range(3):
            at = end + k * HALO
            lines += [ref[at + i : at + i + 1] for i in ((1, 0) if e else (0, 1))]
            lines += [s_ref[k, y : y + 1] for y in ([rows - 1, rows - 2, rows - 3] if e else [0, 1, 2])]
    lines = jnp.concatenate(lines + lines[:2], axis=0) * -(coupling / hopping)
    for t, got in enumerate(moved_exactly(lines, matrix)):
        at = pl.ds(t * 128, 128)
        for e in range(2):
            for k in range(3):
                five = [got[(e * 3 + k) * 5 + i : (e * 3 + k) * 5 + i + 1] for i in range(5)]
                for i, row in enumerate(five + [five[1] + five[2] + five[3] + five[4]]):
                    sp_ref[e, i, k, :, at] = jnp.broadcast_to(row, (LANES, 128))
    for e, ref in enumerate((low_ref, high_ref)):
        for t, got in enumerate(moved(ref[:end].astype(jnp.bfloat16), matrix)):
            got = got.reshape(HALO, 4, parts, LANES, 128)
            for g in range(parts):
                halo_ref[g, e, :, :, :, t * 128 : (t + 1) * 128] = got[:, :, g]

    for e, ref in enumerate(g_refs):
        sums = [None] * tiles
        for g in range(parts):
            own = lambda i: (kept_ref, (g, e, i - 1))
            b1, b2 = (halo_ref, (g, e, 0)), (halo_ref, (g, e, 1))
            a3 = by_tile(own(3))
            sides = [beside([x[k] for x in a3]) for k in range(4)]
            for t in range(tiles):
                w = on_site(a3[t], load(sp_ref, (e, SPINS.index("B1 to A3")), t), ratio)
                w = plus(w, times(4.0, [x[t] for x in sides]), load(*own(4), t))
                here = density(load(*b1, t), w) + density(load(*b2, t), a3[t])
                sums[t] = here if g == 0 else plus(sums[t], here)
        for t, x in enumerate(sums):
            rows_out = [x[i * 3 + k] for k in range(3) for i in (range(HALO) if e else reversed(range(HALO)))]
            ref[:, t * 128 : (t + 1) * 128] = side_by_side(rows_out + rows_out[:2])


def cross(part, kept_ref, sp_ref, halo_ref, mid_ref, acc_ref, old_ref, rho):
    tiles = halo_ref.shape[-1] // 128

    @pl.loop(0, 2)
    def _(e):
        spin = lambda name: (sp_ref, (e, SPINS.index(name)))
        own = lambda i: (kept_ref, (part, e, i - 1))
        a_in, b_in = (kept_ref, (part, e, REACH)), (kept_ref, (part, e, REACH + 1))
        b1, b2 = (halo_ref, (part, e, 0)), (halo_ref, (part, e, 1))
        names = ("a_b2", "a_b1", "b_b2", "b_b1", "b_a1", "c_b1", "c_a1", "c_a2")
        mid = {name: (mid_ref, (i,)) for i, name in enumerate(names)}

        def make(row, at, others, ratio=None, extra=None):
            for t, x in flat(by_tile(row), spin(at), ratio):
                for ref, place in others:
                    x = plus(x, load(ref, place, t))
                if extra is not None:
                    x = plus(x, times(extra[0], load(*extra[1], t)))
                yield t, x

        def state(name, *rest, **more):
            for t, x in make(*rest, **more):
                save(*mid[name], t, x)

        def fields(i, r, w):
            for t, x in w:
                x = density(load(*r, t), x)
                if old_ref is not None:
                    x = plus(x, load(old_ref, (e, i), t))
                save(acc_ref, (e, i), t, x)

        state("a_b2", b2, "B2", [b1], ratio=rho[3])
        state("a_b1", b1, "B1", [b2, own(1)], ratio=rho[3])
        state("b_b2", mid["a_b2"], "B2", [mid["a_b1"], b2], extra=(rho[2], b2))
        state("b_b1", mid["a_b1"], "B1", [mid["a_b2"], a_in, b1], extra=(rho[2], b1))
        state("b_a1", b1, "A1", [mid["a_b1"]])
        state("c_b1", mid["b_b1"], "B1", [mid["b_b2"], b_in, mid["b_a1"]], extra=(rho[1], b1))
        state("c_a1", mid["b_a1"], "A1", [mid["b_b1"], b1])
        state("c_a2", b1, "A2", [mid["b_a1"]])
        fields(0, own(1), make(mid["c_a1"], "A1", [mid["c_b1"], mid["c_a2"]]))
        fields(1, own(2), make(mid["c_a2"], "A2", [mid["c_a1"], b1]))
        fields(2, own(3), make(b1, "A3", [mid["c_a2"]]))
        fields(3, own(4), ((t, load(*b1, t)) for t in range(tiles)))


def begin_kernel(coef_ref, kept_ref, low_ref, high_ref, s_ref, there_ref, sp_ref, halo_ref, g_low_ref, g_high_ref, acc_ref, mid_ref):
    rho = ratios(coef_ref)
    prepare(kept_ref, low_ref, high_ref, s_ref, there_ref, sp_ref, halo_ref, (g_low_ref, g_high_ref), rho[3])
    cross(0, kept_ref, sp_ref, halo_ref, mid_ref, acc_ref, None, rho)


def begin(coefficients, kept, low, high, spins, there):
    f32 = jnp.float32
    parts, width = kept.shape[0], spins.shape[-1]
    out = [
        (2, len(SPINS), 3, LANES, width),
        (parts, 2, HALO, 4, LANES, width),
        (8, width),
        (8, width),
        (2, REACH, 3, LANES, width),
    ]
    vmem = pl.BlockSpec(memory_space=pltpu.VMEM)
    return pl.pallas_call(
        begin_kernel,
        in_specs=[pl.BlockSpec(memory_space=pltpu.SMEM)] + [vmem] * 5,
        out_specs=[vmem] * len(out),
        out_shape=[jax.ShapeDtypeStruct(x, f32) for x in out],
        scratch_shapes=[pltpu.VMEM((8, 4, LANES, width), f32)],
        compiler_params=pltpu.CompilerParams(vmem_limit_bytes=32 * MIB),
        cost_estimate=pl.CostEstimate(flops=500 * low.size, bytes_accessed=4 * MIB, transcendentals=0),
        name="begin",
    )(coefficients, kept, low, high, spins, there)


def end_kernel(coef_ref, kept_ref, sp_ref, halo_ref, old_ref, f_ref, out_ref, mid_ref, acc_ref):
    _, rows, width = f_ref.shape
    parts = kept_ref.shape[0]
    rho = ratios(coef_ref)
    for part in range(1, parts):
        cross(part, kept_ref, sp_ref, halo_ref, mid_ref, acc_ref, old_ref if part == 1 else acc_ref, rho)
    last_ref = acc_ref if parts > 1 else old_ref
    out_ref[...] = f_ref[...]
    half = lax.broadcasted_iota(jnp.int32, (8, 128), 0) < REACH
    for t in range(width // 128):
        at = pl.ds(t * 128, 128)
        for k in range(3):
            low = [last_ref[0, i, k, :, at] for i in range(REACH)]
            high = [last_ref[1, i, k, :, at] for i in reversed(range(REACH))]
            edge = side_by_side(low + high)
            out_ref[k, :8, at] += jnp.where(half, edge, 0.0)
            out_ref[k, rows - 8 :, at] += jnp.where(half, 0.0, edge)


def end(coefficients, kept, sp, halo, old, f):
    f32 = jnp.float32
    vmem = pl.BlockSpec(memory_space=pltpu.VMEM)
    return pl.pallas_call(
        end_kernel,
        in_specs=[pl.BlockSpec(memory_space=pltpu.SMEM)] + [vmem] * 5,
        out_specs=vmem,
        out_shape=jax.ShapeDtypeStruct(f.shape, f32),
        scratch_shapes=[pltpu.VMEM((8, 4, LANES, f.shape[-1]), f32), pltpu.VMEM(old.shape, f32)],
        compiler_params=pltpu.CompilerParams(vmem_limit_bytes=32 * MIB),
        cost_estimate=pl.CostEstimate(flops=300 * kept.size, bytes_accessed=3 * MIB, transcendentals=0),
        name="end",
    )(coefficients, kept, sp, halo, old, f)


def sine_and_cosine(x):
    quarters = jnp.floor(x * (2.0 / jnp.pi) + 0.5)
    for part in (1.5703125, 4.837512969970703125e-4, 7.54978995489188216e-8):
        x = x - quarters * part
    z = x * x
    sine = ((-1.9515295891e-4 * z + 8.3321608736e-3) * z - 1.6666654611e-1) * z * x + x
    cosine = ((2.443315711809948e-5 * z - 1.388731625493765e-3) * z + 4.166664568298827e-2) * z * z - 0.5 * z + 1.0
    turns = quarters.astype(jnp.int32)
    odd, half = (turns & 1) == 1, (turns & 2) == 2
    sine, cosine = jnp.where(odd, cosine, sine), jnp.where(odd, -sine, cosine)
    return jnp.where(half, -sine, sine), jnp.where(half, -cosine, cosine)


def final_kernel(count_all, coef_ref, s_ref, back_ref, f_ref, other_ref, rotated_ref, fields_ref):
    _, rows, width = s_ref.shape
    total = f_ref[...] + other_ref[...]
    scale = ratios(coef_ref)[4][:1, :1] * (coupling / count_all)
    got = moved_exactly(total.reshape(3 * rows, width), back_ref[...])
    for t, x in enumerate(got):
        at = pl.ds(t * 128, 128)
        field = [x[k * rows : (k + 1) * rows] * scale for k in range(3)]
        spin = [s_ref[k, :, at] for k in range(3)]
        size = jnp.sqrt(field[0] * field[0] + field[1] * field[1] + field[2] * field[2])
        half_angle = (0.5 * time_step) * size
        sine, cosine = sine_and_cosine(half_angle)
        some = half_angle > 0.0
        ratio = jnp.where(some, sine / jnp.where(some, half_angle, 1.0), 1.0)
        along = field[0] * spin[0] + field[1] * spin[1] + field[2] * spin[2]
        keep = 1.0 - 2.0 * sine * sine
        turn = time_step * ratio * cosine
        lift = (0.5 * time_step * time_step) * ratio * ratio * along
        for k in range(3):
            i, j = (k + 1) % 3, (k + 2) % 3
            cross = field[i] * spin[j] - field[j] * spin[i]
            rotated_ref[k, :, at] = keep * spin[k] + turn * cross + lift * field[k]
            fields_ref[k, :, at] = field[k]


def final(coefficients, spins, back, count_all, f, other):
    out = jax.ShapeDtypeStruct(spins.shape, jnp.float32)
    vmem = pl.BlockSpec(memory_space=pltpu.VMEM)
    return pl.pallas_call(
        functools.partial(final_kernel, count_all),
        in_specs=[pl.BlockSpec(memory_space=pltpu.SMEM)] + [vmem] * 4,
        out_specs=[vmem] * 2,
        out_shape=[out, out],
        compiler_params=pltpu.CompilerParams(vmem_limit_bytes=32 * MIB),
        name="final",
    )(coefficients, spins, back, f, other)


def shards(vectors, classical_spins, coefficients):
    across, number = lax.axis_size("vec"), lax.axis_size("lat")
    count_all = vectors.shape[1] * across

    def to_row(x, on):
        return lax.ppermute(x, "lat", [(i, (i + on) % number) for i in range(number)])

    def swap(x, step):
        steps = across.bit_length() - 1
        bit = lambda i: 1 << (step if i % 2 == 0 else steps - 1 - step)
        pairs = [(i * across + j, i * across + (j ^ bit(i))) for i in range(number) for j in range(across)]
        return lax.ppermute(x, ("lat", "vec"), pairs)

    rows, width = classical_spins.shape[1:]
    low, high, vectors, spins = edges(vectors, classical_spins)
    from_below, from_above = to_row(high, 1), to_row(low, -1)
    f, kept, there, back = inner(coefficients, vectors, spins)
    sp, halo, g_low, g_high, crossed = begin(coefficients, kept, from_below, from_above, spins, there)
    below, above = to_row(g_high, 1), to_row(g_low, -1)
    fields = end(coefficients, kept, sp, halo, crossed, f)
    lines = lambda x: x[: 3 * HALO].reshape(3, HALO, width)
    fields = fields.at[:, :HALO].add(lines(below)).at[:, rows - HALO :].add(lines(above))
    steps = across.bit_length() - 1
    if across != 1 << steps or steps == 0:
        return final(coefficients, spins, back, count_all, lax.psum(fields, "vec"), jnp.zeros_like(fields))
    for step in range(steps - 1):
        fields = fields + swap(fields, step)
    return final(coefficients, spins, back, count_all, fields, swap(fields, steps - 1))


def solution(mesh):
    placed = (P(None, "vec", "lat", None), P(None, "lat", None), P())
    return jax.shard_map(
        shards,
        mesh=mesh,
        in_specs=placed,
        out_specs=(P(None, "lat", None), P(None, "lat", None)),
        check_vma=False,
    )
```

```python
import functools

import jax
import jax.numpy as jnp
from jax import lax
from jax.experimental import pallas as pl
from jax.experimental.pallas import tpu as pltpu
from jax.sharding import PartitionSpec as P

coupling = 2.0
hopping = 1.0
inverse_bound = 1.0 / 6.5
time_step = 1.0

LANES = 8
REACH = 4
HALO = 2
MIB = 1 << 20


def inwards(odd, side, i, rows):
    high = odd if side == 0 else 1 - odd
    return i + high * (rows - 1 - 2 * i)


def ratios(coefs):
    step = -hopping * inverse_bound
    c = [jnp.full((LANES, 128), coefs[k], jnp.float32) for k in range(5)]
    top = c[4] * (8.0 * step**4)
    under = 1.0 / top
    return [
        (c[0] - c[2] + c[4]) * under,
        (c[1] - 3.0 * c[3]) * step * under,
        (2.0 * c[2] - 8.0 * c[4]) * step**2 * under,
        4.0 * c[3] * step**3 * under,
        top,
    ]


def block_of(width):
    return next(b for b in (512, 256, 128) if width % b == 0)


def shuffle(width, back=False):
    block = block_of(width)
    tiles = block // 128
    source = lax.broadcasted_iota(jnp.int32, (block, block), 1 if back else 0)
    target = lax.broadcasted_iota(jnp.int32, (block, block), 0 if back else 1)
    place = lax.rem(source, tiles) * 128 + lax.div(source, tiles)
    return (place == target).astype(jnp.float32).astype(jnp.bfloat16)


def moved(states, matrix):
    block = matrix.shape[0]
    out = []
    for at in range(0, states.shape[1], block):
        got = jnp.dot(states[:, at : at + block], matrix, preferred_element_type=jnp.float32)
        out += [got[:, t : t + 128] for t in range(0, block, 128)]
    return out


def moved_exactly(rows, matrix):
    parts = []
    for _ in range(3):
        parts.append(rows.astype(jnp.bfloat16))
        rows = rows - parts[-1].astype(jnp.float32)
    count = rows.shape[0]
    got = moved(jnp.concatenate(parts, axis=0), matrix)
    return [x[:count] + x[count : 2 * count] + x[2 * count :] for x in got]


def on_left(tiles):
    group = block_of(len(tiles) * 128) // 128
    lane = lax.broadcasted_iota(jnp.int32, tiles[0].shape, 1)
    ends = [pltpu.roll(x, 1, 1) for x in tiles[group - 1 :: group]]
    if len(ends) > 1:
        ends = [jnp.where(lane == 0, ends[b - 1], x) for b, x in enumerate(ends)]
    return [tiles[t - 1] if t % group else ends[t // group] for t in range(len(tiles))]


def on_right(tiles):
    group = block_of(len(tiles) * 128) // 128
    lane = lax.broadcasted_iota(jnp.int32, tiles[0].shape, 1)
    starts = [pltpu.roll(x, 127, 1) for x in tiles[::group]]
    if len(starts) > 1:
        starts = [jnp.where(lane == 127, starts[(b + 1) % len(starts)], x) for b, x in enumerate(starts)]
    return [tiles[t + 1] if (t + 1) % group else starts[t // group] for t in range(len(tiles))]


def beside(tiles):
    return [x + y for x, y in zip(on_left(tiles), on_right(tiles))]


def on_site(state, spins, ratio=None):
    sx, sy, sz = spins
    ur, ui, dr, di = state
    zp, zm = (sz, sz) if ratio is None else (sz + ratio, sz - ratio)
    return [
        zp * ur + sx * dr + sy * di,
        zp * ui + sx * di - sy * dr,
        sx * ur - sy * ui - zm * dr,
        sx * ui + sy * ur - zm * di,
    ]


def density(r, w):
    return [
        r[0] * w[2] + r[1] * w[3] + r[2] * w[0] + r[3] * w[1],
        r[0] * w[3] - r[1] * w[2] - r[2] * w[1] + r[3] * w[0],
        r[0] * w[0] + r[1] * w[1] - r[2] * w[2] - r[3] * w[3],
    ]


def plus(*states):
    return [functools.reduce(lambda a, b: a + b, parts) for parts in zip(*states)]


def times(ratio, state):
    return [ratio * x for x in state]


def load(ref, at, t):
    return [ref[(*at, k, slice(None), pl.ds(t * 128, 128))] for k in range(ref.shape[len(at)])]


def save(ref, at, t, state):
    for k, x in enumerate(state):
        ref[(*at, k, slice(None), pl.ds(t * 128, 128))] = x


def by_tile(row):
    ref, at = row
    return [load(ref, at, t) for t in range(ref.shape[-1] // 128)]


def lateral(row):
    return [beside([x[k] for x in row]) for k in range(4)]


def flat(row, spin, ratio=None, sides=None):
    sides = sides or lateral(row)
    for t, here in enumerate(row):
        yield t, plus([x[t] for x in sides], on_site(here, load(*spin, t), ratio))


def side_by_side(tiles):
    sub = lax.broadcasted_iota(jnp.int32, tiles[0].shape, 0)
    apart = 4
    while apart:
        first = (sub & apart) == 0
        tiles = [
            jnp.where(first, x + pltpu.roll(x, 8 - apart, 0), y + pltpu.roll(y, apart, 0))
            for x, y in zip(tiles[: len(tiles) // 2], tiles[len(tiles) // 2 :])
        ]
        apart //= 2
    return tiles[0]


def edges_kernel(odd_ref, v_hbm, s_hbm, far_ref, near_ref, v_ref, s_ref, rows_ref, v_sem, s_sem):
    _, count, rows, width = v_hbm.shape
    odd = odd_ref[0]
    copies = [pltpu.make_async_copy(v_hbm.at[comp], v_ref.at[comp], v_sem.at[comp]) for comp in range(4)]
    for copy in copies:
        copy.start()
    spins = pltpu.make_async_copy(s_hbm, s_ref, s_sem)
    spins.start()
    for comp in range(4):
        copies[comp].wait()
        for g in range(count // LANES):
            states = v_ref[comp, g * LANES : (g + 1) * LANES].astype(jnp.float32).reshape(LANES * rows, width)
            for t in range(width // 128):
                rows_ref[comp, g, t] = states[:, t * 128 : (t + 1) * 128]
            for i in range(HALO):
                to = pl.ds((i * 4 + comp) * count + g * LANES, LANES)
                for t in range(width // 128):
                    at = pl.ds(t * 128, 128)
                    for side, ref in enumerate((far_ref, near_ref)):
                        ref[to, at] = rows_ref[comp, g, t, pl.ds(inwards(odd, side, i, rows), LANES, stride=rows), :]
    spins.wait()
    end = HALO * 4 * count
    for side, ref in enumerate((far_ref, near_ref)):
        lines = [s_ref[k, pl.ds(inwards(odd, side, i, rows), 1)] for k in range(3) for i in range(HALO)]
        ref[end:] = jnp.concatenate(lines + lines[: 8 - 3 * HALO], axis=0)


def edges(odd, vectors, spins):
    _, count, rows, width = vectors.shape
    f32 = jnp.float32
    out = pltpu.VMEM((HALO * 4 * count + 8, width), f32)
    hbm, vmem = pl.BlockSpec(memory_space=pltpu.HBM), pl.BlockSpec(memory_space=pltpu.VMEM)
    return pl.pallas_call(
        edges_kernel,
        in_specs=[pl.BlockSpec(memory_space=pltpu.SMEM)] + [hbm] * 2,
        out_specs=[vmem] * 4,
        out_shape=[out, out, pltpu.VMEM(vectors.shape, vectors.dtype), pltpu.VMEM(spins.shape, f32)],
        scratch_shapes=[
            pltpu.VMEM((4, count // LANES, width // 128, LANES * rows, 128), f32),
            pltpu.SemaphoreType.DMA((4,)),
            pltpu.SemaphoreType.DMA,
        ],
        compiler_params=pltpu.CompilerParams(vmem_limit_bytes=16 * MIB),
        name="edges",
    )(odd, *[pltpu.with_memory_space_constraint(x, pltpu.HBM) for x in (vectors, spins)])


KEPT = REACH + 2
GROUP = 8


def inner_kernel(odd_ref, coef_ref, v_ref, s_ref, f_ref, kept_ref, there_ref, back_ref, rows_ref, r_ref, sp_ref, a_ref, b_ref, sum_ref, acc_ref):
    _, count, rows, width = v_ref.shape
    tiles = width // 128
    odd = odd_ref[0]
    rho = ratios(coef_ref)

    there_ref[...] = shuffle(width)
    acc_ref[...] = jnp.zeros_like(acc_ref)
    for ref in (r_ref, a_ref, b_ref):
        ref[rows] = jnp.zeros(ref.shape[1:], jnp.float32)
    spins = s_ref[...].reshape(3 * rows, width) * -(coupling / hopping)
    for t, got in enumerate(moved_exactly(spins, there_ref[...])):
        for y in range(rows):
            for k in range(3):
                row = got[k * rows + y : k * rows + y + 1]
                sp_ref[y, k, :, t * 128 : (t + 1) * 128] = jnp.broadcast_to(row, (LANES, 128))

    def pass_over(dst, src, ratio, own=False):
        sum_ref[...] = src[0]

        @pl.loop(0, rows, step=GROUP)
        def _(start):
            below = [[sum_ref[k, :, t * 128 : (t + 1) * 128] for t in range(tiles)] for k in range(4)]
            for y in [start + i for i in range(GROUP)]:
                here = by_tile((src, (y,)))
                pairs = []
                for k in range(4):
                    right = on_right([x[k] for x in here])
                    pairs.append([right[t] + src[y + 1, k, :, t * 128 : (t + 1) * 128] for t in range(tiles)])
                left = [on_left(x) for x in below]
                for t in range(tiles):
                    x = plus([x[t] for x in pairs], [x[t] for x in left])
                    x = plus(x, on_site(here[t], load(sp_ref, (y,), t), ratio if own else None))
                    if not own:
                        x = plus(x, times(ratio, load(r_ref, (y,), t)))
                    dst(y, t, x)
                below = pairs
            for k in range(4):
                for t in range(tiles):
                    sum_ref[k, :, t * 128 : (t + 1) * 128] = below[k][t]

    def into(ref):
        return lambda y, t, x: save(ref, (y,), t, x)

    def fields(y, t, w):
        save(acc_ref, (y,), t, plus(density(load(r_ref, (y,), t), w), load(acc_ref, (y,), t)))

    @pl.loop(0, count // LANES)
    def _(g):
        states = v_ref[:, pl.ds(pl.multiple_of(g * LANES, LANES), LANES)]
        for t, got in enumerate(moved(states.reshape(4 * LANES * rows, width), there_ref[...])):
            rows_ref[t] = got

        for y in range(rows):
            for comp in range(4):
                for t in range(tiles):
                    at = pl.ds(comp * LANES * rows + y, LANES, stride=rows)
                    r_ref[y, comp, :, t * 128 : (t + 1) * 128] = rows_ref[t, at, :]

        pass_over(into(a_ref), r_ref, rho[3], own=True)
        pass_over(into(b_ref), a_ref, rho[2])
        for side in range(2):
            for i in range(REACH):
                kept_ref[g, side, i] = r_ref[inwards(odd, side, i, rows)]
            kept_ref[g, side, REACH] = a_ref[inwards(odd, side, 0, rows)]
            kept_ref[g, side, REACH + 1] = b_ref[inwards(odd, side, 0, rows)]
        pass_over(into(a_ref), b_ref, rho[1])
        pass_over(fields, a_ref, rho[0])

    for k in range(3):
        for y in range(0, rows, 8):
            for t in range(tiles):
                at = pl.ds(t * 128, 128)
                f_ref[k, y : y + 8, at] = side_by_side([acc_ref[y + i, k, :, at] for i in range(8)])
    back_ref[...] = shuffle(width, back=True)


def inner(odd, coefficients, vectors, spins):
    _, count, rows, width = vectors.shape
    f32 = jnp.float32
    block = block_of(width)
    matrix = jax.ShapeDtypeStruct((block, block), jnp.bfloat16)
    state = pltpu.VMEM((rows + 1, 4, LANES, width), f32)
    vmem = pl.BlockSpec(memory_space=pltpu.VMEM)
    return pl.pallas_call(
        inner_kernel,
        in_specs=[pl.BlockSpec(memory_space=pltpu.SMEM)] * 2 + [vmem] * 2,
        out_specs=[vmem] * 4,
        out_shape=[
            jax.ShapeDtypeStruct((3, rows, width), f32),
            jax.ShapeDtypeStruct((count // LANES, 2, KEPT, 4, LANES, width), f32),
            matrix,
            matrix,
        ],
        scratch_shapes=[
            pltpu.VMEM((width // 128, 4 * LANES * rows, 128), f32),
            state,
            pltpu.VMEM((rows, 3, LANES, width), f32),
            state,
            state,
            pltpu.VMEM((4, LANES, width), f32),
            pltpu.VMEM((rows, 3, LANES, width), f32),
        ],
        compiler_params=pltpu.CompilerParams(vmem_limit_bytes=40 * MIB),
        cost_estimate=pl.CostEstimate(flops=240 * vectors.size, bytes_accessed=8 * MIB, transcendentals=0),
        name="inner",
    )(odd, coefficients, vectors, spins)


SPINS = ("B2", "B1", "A1", "A2", "A3", "B1 to A3")


def prepare(odd, kept_ref, far_ref, near_ref, s_ref, there_ref, sp_ref, halo_ref, g_refs, ratio):
    _, rows, width = s_ref.shape
    parts = kept_ref.shape[0]
    tiles = width // 128
    end = HALO * 4 * parts * LANES
    matrix = there_ref[...]
    lines = []
    for e, ref in enumerate((far_ref, near_ref)):
        for k in range(3):
            at = end + k * HALO
            lines += [ref[at + i : at + i + 1] for i in (1, 0)]
            lines += [s_ref[k, pl.ds(inwards(odd, e, i, rows), 1)] for i in range(3)]
    lines = jnp.concatenate(lines + lines[:2], axis=0) * -(coupling / hopping)
    for t, got in enumerate(moved_exactly(lines, matrix)):
        at = pl.ds(t * 128, 128)
        for e in range(2):
            for k in range(3):
                five = [got[(e * 3 + k) * 5 + i : (e * 3 + k) * 5 + i + 1] for i in range(5)]
                for i, row in enumerate(five + [five[1] + five[2] + five[3] + five[4]]):
                    sp_ref[e, i, k, :, at] = jnp.broadcast_to(row, (LANES, 128))
    for e, ref in enumerate((far_ref, near_ref)):
        for t, got in enumerate(moved(ref[:end].astype(jnp.bfloat16), matrix)):
            got = got.reshape(HALO, 4, parts, LANES, 128)
            for g in range(parts):
                halo_ref[g, e, :, :, :, t * 128 : (t + 1) * 128] = got[:, :, g]

    for e, ref in enumerate(g_refs):
        sums = [None] * tiles
        for g in range(parts):
            own = lambda i: (kept_ref, (g, e, i - 1))
            b1, b2 = (halo_ref, (g, e, 0)), (halo_ref, (g, e, 1))
            a3 = by_tile(own(3))
            sides = [beside([x[k] for x in a3]) for k in range(4)]
            for t in range(tiles):
                w = on_site(a3[t], load(sp_ref, (e, SPINS.index("B1 to A3")), t), ratio)
                w = plus(w, times(4.0, [x[t] for x in sides]), load(*own(4), t))
                here = density(load(*b1, t), w) + density(load(*b2, t), a3[t])
                sums[t] = here if g == 0 else plus(sums[t], here)
        low = (odd if e == 0 else 1 - odd).astype(jnp.float32)
        zero = jnp.zeros((LANES, 128), jnp.float32)
        for t, x in enumerate(sums):
            at = pl.ds(t * 128, 128)
            ref[:8, at] = low * side_by_side([x[i * 3 + k] for k in range(3) for i in range(HALO)] + [zero] * 2)
            ref[8:, at] = (1.0 - low) * side_by_side([x[i * 3 + k] for k in range(3) for i in (1, 0)] + [zero] * 2)


def cross(part, kept_ref, sp_ref, halo_ref, mid_ref, acc_ref, old_ref, rho):
    tiles = halo_ref.shape[-1] // 128

    @pl.loop(0, 2)
    def _(e):
        spin = lambda name: (sp_ref, (e, SPINS.index(name)))
        own = lambda i: (kept_ref, (part, e, i - 1))
        a_in, b_in = (kept_ref, (part, e, REACH)), (kept_ref, (part, e, REACH + 1))
        b1, b2 = (halo_ref, (part, e, 0)), (halo_ref, (part, e, 1))
        names = ("a_b2", "a_b1", "b_b2", "b_b1", "b_a1", "c_b1", "c_a1", "c_a2", "b1_sides")
        mid = {name: (mid_ref, (i,)) for i, name in enumerate(names)}
        b1_sides = mid["b1_sides"]

        b1_tiles = by_tile(b1)
        for t, x in enumerate(zip(*lateral(b1_tiles))):
            save(*b1_sides, t, x)

        def make(row, at, others, ratio=None, extra=None):
            if row is b1:
                made = ((t, plus(load(*b1_sides, t), on_site(load(*b1, t), load(*spin(at), t), ratio))) for t in range(tiles))
            else:
                made = flat(by_tile(row), spin(at), ratio)
            for t, x in made:
                for ref, place in others:
                    x = plus(x, load(ref, place, t))
                if extra is not None:
                    x = plus(x, times(extra[0], load(*extra[1], t)))
                yield t, x

        def state(name, *rest, **more):
            for t, x in make(*rest, **more):
                save(*mid[name], t, x)

        def fields(i, r, w):
            for t, x in w:
                x = density(load(*r, t), x)
                if old_ref is not None:
                    x = plus(x, load(old_ref, (e, i), t))
                save(acc_ref, (e, i), t, x)

        state("a_b2", b2, "B2", [b1], ratio=rho[3])
        state("a_b1", b1, "B1", [b2, own(1)], ratio=rho[3])
        state("b_b2", mid["a_b2"], "B2", [mid["a_b1"], b2], extra=(rho[2], b2))
        state("b_b1", mid["a_b1"], "B1", [mid["a_b2"], a_in, b1], extra=(rho[2], b1))
        state("b_a1", b1, "A1", [mid["a_b1"]])
        state("c_b1", mid["b_b1"], "B1", [mid["b_b2"], b_in, mid["b_a1"]], extra=(rho[1], b1))
        state("c_a1", mid["b_a1"], "A1", [mid["b_b1"], b1])
        state("c_a2", b1, "A2", [mid["b_a1"]])
        fields(0, own(1), make(mid["c_a1"], "A1", [mid["c_b1"], mid["c_a2"]]))
        fields(1, own(2), make(mid["c_a2"], "A2", [mid["c_a1"], b1]))
        fields(2, own(3), make(b1, "A3", [mid["c_a2"]]))
        fields(3, own(4), ((t, load(*b1, t)) for t in range(tiles)))


def begin_kernel(odd_ref, coef_ref, kept_ref, far_ref, near_ref, s_ref, there_ref, sp_ref, halo_ref, g_far_ref, g_near_ref):
    rho = ratios(coef_ref)
    prepare(odd_ref[0], kept_ref, far_ref, near_ref, s_ref, there_ref, sp_ref, halo_ref, (g_far_ref, g_near_ref), rho[3])


def begin(odd, coefficients, kept, far, near, spins, there):
    f32 = jnp.float32
    parts, width = kept.shape[0], spins.shape[-1]
    out = [
        (2, len(SPINS), 3, LANES, width),
        (parts, 2, HALO, 4, LANES, width),
        (16, width),
        (16, width),
    ]
    vmem = pl.BlockSpec(memory_space=pltpu.VMEM)
    return pl.pallas_call(
        begin_kernel,
        in_specs=[pl.BlockSpec(memory_space=pltpu.SMEM)] * 2 + [vmem] * 5,
        out_specs=[vmem] * len(out),
        out_shape=[jax.ShapeDtypeStruct(x, f32) for x in out],
        compiler_params=pltpu.CompilerParams(vmem_limit_bytes=32 * MIB),
        cost_estimate=pl.CostEstimate(flops=500 * far.size, bytes_accessed=4 * MIB, transcendentals=0),
        name="begin",
    )(odd, coefficients, kept, far, near, spins, there)


def end_kernel(odd_ref, coef_ref, kept_ref, sp_ref, halo_ref, f_ref, out_ref, mid_ref, acc_ref):
    _, rows, width = f_ref.shape
    parts = kept_ref.shape[0]
    rho = ratios(coef_ref)
    for part in range(parts):
        cross(part, kept_ref, sp_ref, halo_ref, mid_ref, acc_ref, acc_ref if part else None, rho)
    out_ref[...] = f_ref[...]
    half = lax.broadcasted_iota(jnp.int32, (8, 128), 0) < REACH
    for t in range(width // 128):
        at = pl.ds(t * 128, 128)
        for k in range(3):
            low = [acc_ref[odd_ref[0], i, k, :, at] for i in range(REACH)]
            high = [acc_ref[1 - odd_ref[0], i, k, :, at] for i in reversed(range(REACH))]
            edge = side_by_side(low + high)
            out_ref[k, :8, at] += jnp.where(half, edge, 0.0)
            out_ref[k, rows - 8 :, at] += jnp.where(half, 0.0, edge)


def end(odd, coefficients, kept, sp, halo, f):
    f32 = jnp.float32
    vmem = pl.BlockSpec(memory_space=pltpu.VMEM)
    return pl.pallas_call(
        end_kernel,
        in_specs=[pl.BlockSpec(memory_space=pltpu.SMEM)] * 2 + [vmem] * 4,
        out_specs=vmem,
        out_shape=jax.ShapeDtypeStruct(f.shape, f32),
        scratch_shapes=[pltpu.VMEM((9, 4, LANES, f.shape[-1]), f32), pltpu.VMEM((2, REACH, 3, LANES, f.shape[-1]), f32)],
        compiler_params=pltpu.CompilerParams(vmem_limit_bytes=32 * MIB),
        cost_estimate=pl.CostEstimate(flops=300 * kept.size, bytes_accessed=3 * MIB, transcendentals=0),
        name="end",
    )(odd, coefficients, kept, sp, halo, f)


def sine_and_cosine(x):
    quarters = jnp.floor(x * (2.0 / jnp.pi) + 0.5)
    for part in (1.5703125, 4.837512969970703125e-4, 7.54978995489188216e-8):
        x = x - quarters * part
    z = x * x
    sine = ((-1.9515295891e-4 * z + 8.3321608736e-3) * z - 1.6666654611e-1) * z * x + x
    cosine = ((2.443315711809948e-5 * z - 1.388731625493765e-3) * z + 4.166664568298827e-2) * z * z - 0.5 * z + 1.0
    turns = quarters.astype(jnp.int32)
    odd, half = (turns & 1) == 1, (turns & 2) == 2
    sine, cosine = jnp.where(odd, cosine, sine), jnp.where(odd, -sine, cosine)
    return jnp.where(half, -sine, sine), jnp.where(half, -cosine, cosine)


def final_kernel(count_all, coef_ref, s_ref, back_ref, f_ref, other_ref, rotated_ref, fields_ref):
    _, rows, width = s_ref.shape
    total = f_ref[...] + other_ref[...]
    scale = ratios(coef_ref)[4][:1, :1] * (coupling / count_all)
    got = moved_exactly(total.reshape(3 * rows, width), back_ref[...])
    for t, x in enumerate(got):
        at = pl.ds(t * 128, 128)
        field = [x[k * rows : (k + 1) * rows] * scale for k in range(3)]
        spin = [s_ref[k, :, at] for k in range(3)]
        size = jnp.sqrt(field[0] * field[0] + field[1] * field[1] + field[2] * field[2])
        half_angle = (0.5 * time_step) * size
        sine, cosine = sine_and_cosine(half_angle)
        some = half_angle > 0.0
        ratio = jnp.where(some, sine / jnp.where(some, half_angle, 1.0), 1.0)
        along = field[0] * spin[0] + field[1] * spin[1] + field[2] * spin[2]
        keep = 1.0 - 2.0 * sine * sine
        turn = time_step * ratio * cosine
        lift = (0.5 * time_step * time_step) * ratio * ratio * along
        for k in range(3):
            i, j = (k + 1) % 3, (k + 2) % 3
            cross = field[i] * spin[j] - field[j] * spin[i]
            rotated_ref[k, :, at] = keep * spin[k] + turn * cross + lift * field[k]
            fields_ref[k, :, at] = field[k]


def final(coefficients, spins, back, count_all, f, other):
    out = jax.ShapeDtypeStruct(spins.shape, jnp.float32)
    vmem = pl.BlockSpec(memory_space=pltpu.VMEM)
    return pl.pallas_call(
        functools.partial(final_kernel, count_all),
        in_specs=[pl.BlockSpec(memory_space=pltpu.SMEM)] + [vmem] * 4,
        out_specs=[vmem] * 2,
        out_shape=[out, out],
        compiler_params=pltpu.CompilerParams(vmem_limit_bytes=32 * MIB),
        name="final",
    )(coefficients, spins, back, f, other)


def shards(vectors, classical_spins, coefficients):
    across, number = lax.axis_size("vec"), lax.axis_size("lat")
    count_all = vectors.shape[1] * across

    def trade(x, side):
        return lax.ppermute(x, "lat", [(i, (i + (1 if i % 2 != side else -1)) % number) for i in range(number)])

    def swap(x, step):
        steps = across.bit_length() - 1
        bit = lambda i: 1 << (step if i % 2 == 0 else steps - 1 - step)
        pairs = [(i * across + j, i * across + (j ^ bit(i))) for i in range(number) for j in range(across)]
        return lax.ppermute(x, ("lat", "vec"), pairs)

    rows, width = classical_spins.shape[1:]
    odd = jnp.full((1,), lax.rem(lax.axis_index("lat"), 2), jnp.int32)
    far, near, vectors, spins = edges(odd, vectors, classical_spins)
    far, near = trade(far, 0), trade(near, 1)
    f, kept, there, back = inner(odd, coefficients, vectors, spins)
    sp, halo, g_far, g_near = begin(odd, coefficients, kept, far, near, spins, there)
    g_far, g_near = trade(g_far, 0), trade(g_near, 1)
    fields = end(odd, coefficients, kept, sp, halo, f)
    lines = lambda x: x[: 3 * HALO].reshape(3, HALO, width)
    given = g_far + g_near
    fields = fields.at[:, :HALO].add(lines(given)).at[:, rows - HALO :].add(lines(given[8:]))
    steps = across.bit_length() - 1
    if across != 1 << steps or steps == 0:
        return final(coefficients, spins, back, count_all, lax.psum(fields, "vec"), jnp.zeros_like(fields))
    for step in range(steps - 1):
        fields = fields + swap(fields, step)
    return final(coefficients, spins, back, count_all, fields, swap(fields, steps - 1))


def solution(mesh):
    placed = (P(None, "vec", "lat", None), P(None, "lat", None), P())
    return jax.shard_map(
        shards,
        mesh=mesh,
        in_specs=placed,
        out_specs=(P(None, "lat", None), P(None, "lat", None)),
        check_vma=False,
    )
```

```python
import functools

import jax
import jax.numpy as jnp
from jax import lax
from jax.experimental import pallas as pl
from jax.experimental.pallas import tpu as pltpu
from jax.sharding import PartitionSpec as P

coupling = 2.0
hopping = 1.0
inverse_bound = 1.0 / 6.5
time_step = 1.0

LANES = 8
REACH = 4
HALO = 2
MIB = 1 << 20


def inwards(odd, side, i, rows):
    high = odd if side == 0 else 1 - odd
    return i + high * (rows - 1 - 2 * i)


def ratios(coefs):
    step = -hopping * inverse_bound
    c = [jnp.full((LANES, 128), coefs[k], jnp.float32) for k in range(5)]
    top = c[4] * (8.0 * step**4)
    under = 1.0 / top
    return [
        (c[0] - c[2] + c[4]) * under,
        (c[1] - 3.0 * c[3]) * step * under,
        (2.0 * c[2] - 8.0 * c[4]) * step**2 * under,
        4.0 * c[3] * step**3 * under,
        top,
    ]


def block_of(width):
    return next(b for b in (512, 256, 128) if width % b == 0)


def shuffle(width, back=False):
    block = block_of(width)
    tiles = block // 128
    source = lax.broadcasted_iota(jnp.int32, (block, block), 1 if back else 0)
    target = lax.broadcasted_iota(jnp.int32, (block, block), 0 if back else 1)
    place = lax.rem(source, tiles) * 128 + lax.div(source, tiles)
    return (place == target).astype(jnp.float32).astype(jnp.bfloat16)


def moved(states, matrix):
    block = matrix.shape[0]
    out = []
    for at in range(0, states.shape[1], block):
        got = jnp.dot(states[:, at : at + block], matrix, preferred_element_type=jnp.float32)
        out += [got[:, t : t + 128] for t in range(0, block, 128)]
    return out


def moved_exactly(rows, matrix):
    parts = []
    for _ in range(3):
        parts.append(rows.astype(jnp.bfloat16))
        rows = rows - parts[-1].astype(jnp.float32)
    count = rows.shape[0]
    got = moved(jnp.concatenate(parts, axis=0), matrix)
    return [x[:count] + x[count : 2 * count] + x[2 * count :] for x in got]


def on_left(tiles):
    group = block_of(len(tiles) * 128) // 128
    lane = lax.broadcasted_iota(jnp.int32, tiles[0].shape, 1)
    ends = [pltpu.roll(x, 1, 1) for x in tiles[group - 1 :: group]]
    if len(ends) > 1:
        ends = [jnp.where(lane == 0, ends[b - 1], x) for b, x in enumerate(ends)]
    return [tiles[t - 1] if t % group else ends[t // group] for t in range(len(tiles))]


def on_right(tiles):
    group = block_of(len(tiles) * 128) // 128
    lane = lax.broadcasted_iota(jnp.int32, tiles[0].shape, 1)
    starts = [pltpu.roll(x, 127, 1) for x in tiles[::group]]
    if len(starts) > 1:
        starts = [jnp.where(lane == 127, starts[(b + 1) % len(starts)], x) for b, x in enumerate(starts)]
    return [tiles[t + 1] if (t + 1) % group else starts[t // group] for t in range(len(tiles))]


def beside(tiles):
    return [x + y for x, y in zip(on_left(tiles), on_right(tiles))]


def on_site(state, spins, ratio=None):
    sx, sy, sz = spins
    ur, ui, dr, di = state
    zp, zm = (sz, sz) if ratio is None else (sz + ratio, sz - ratio)
    return [
        zp * ur + sx * dr + sy * di,
        zp * ui + sx * di - sy * dr,
        sx * ur - sy * ui - zm * dr,
        sx * ui + sy * ur - zm * di,
    ]


def density(r, w):
    return [
        r[0] * w[2] + r[1] * w[3] + r[2] * w[0] + r[3] * w[1],
        r[0] * w[3] - r[1] * w[2] - r[2] * w[1] + r[3] * w[0],
        r[0] * w[0] + r[1] * w[1] - r[2] * w[2] - r[3] * w[3],
    ]


def plus(*states):
    return [functools.reduce(lambda a, b: a + b, parts) for parts in zip(*states)]


def times(ratio, state):
    return [ratio * x for x in state]


def load(ref, at, t):
    return [ref[(*at, k, slice(None), pl.ds(t * 128, 128))] for k in range(ref.shape[len(at)])]


def save(ref, at, t, state):
    for k, x in enumerate(state):
        ref[(*at, k, slice(None), pl.ds(t * 128, 128))] = x


def by_tile(row):
    ref, at = row
    return [load(ref, at, t) for t in range(ref.shape[-1] // 128)]


def lateral(row):
    return [beside([x[k] for x in row]) for k in range(4)]


def flat(row, spin, ratio=None, sides=None):
    sides = sides or lateral(row)
    for t, here in enumerate(row):
        yield t, plus([x[t] for x in sides], on_site(here, load(*spin, t), ratio))


def side_by_side(tiles):
    sub = lax.broadcasted_iota(jnp.int32, tiles[0].shape, 0)
    apart = 4
    while apart:
        first = (sub & apart) == 0
        tiles = [
            jnp.where(first, x + pltpu.roll(x, 8 - apart, 0), y + pltpu.roll(y, apart, 0))
            for x, y in zip(tiles[: len(tiles) // 2], tiles[len(tiles) // 2 :])
        ]
        apart //= 2
    return tiles[0]


def edges_kernel(odd_ref, v_hbm, s_hbm, far_ref, near_ref, v_ref, s_ref, rows_ref, v_sem, s_sem):
    _, count, rows, width = v_hbm.shape
    odd = odd_ref[0]
    copies = [pltpu.make_async_copy(v_hbm.at[comp], v_ref.at[comp], v_sem.at[comp]) for comp in range(4)]
    for copy in copies:
        copy.start()
    spins = pltpu.make_async_copy(s_hbm, s_ref, s_sem)
    spins.start()
    for comp in range(4):
        copies[comp].wait()
        for g in range(count // LANES):
            states = v_ref[comp, g * LANES : (g + 1) * LANES].astype(jnp.float32).reshape(LANES * rows, width)
            for t in range(width // 128):
                rows_ref[comp, g, t] = states[:, t * 128 : (t + 1) * 128]
            for i in range(HALO):
                to = pl.ds((i * 4 + comp) * count + g * LANES, LANES)
                for t in range(width // 128):
                    at = pl.ds(t * 128, 128)
                    for side, ref in enumerate((far_ref, near_ref)):
                        ref[to, at] = rows_ref[comp, g, t, pl.ds(inwards(odd, side, i, rows), LANES, stride=rows), :]
    spins.wait()
    end = HALO * 4 * count
    for side, ref in enumerate((far_ref, near_ref)):
        lines = [s_ref[k, pl.ds(inwards(odd, side, i, rows), 1)] for k in range(3) for i in range(HALO)]
        ref[end:] = jnp.concatenate(lines + lines[: 8 - 3 * HALO], axis=0)


def edges(odd, vectors, spins):
    _, count, rows, width = vectors.shape
    f32 = jnp.float32
    out = pltpu.VMEM((HALO * 4 * count + 8, width), f32)
    hbm, vmem = pl.BlockSpec(memory_space=pltpu.HBM), pl.BlockSpec(memory_space=pltpu.VMEM)
    return pl.pallas_call(
        edges_kernel,
        in_specs=[pl.BlockSpec(memory_space=pltpu.SMEM)] + [hbm] * 2,
        out_specs=[vmem] * 4,
        out_shape=[out, out, pltpu.VMEM(vectors.shape, vectors.dtype), pltpu.VMEM(spins.shape, f32)],
        scratch_shapes=[
            pltpu.VMEM((4, count // LANES, width // 128, LANES * rows, 128), f32),
            pltpu.SemaphoreType.DMA((4,)),
            pltpu.SemaphoreType.DMA,
        ],
        compiler_params=pltpu.CompilerParams(vmem_limit_bytes=16 * MIB),
        name="edges",
    )(odd, *[pltpu.with_memory_space_constraint(x, pltpu.HBM) for x in (vectors, spins)])


KEPT = REACH + 2
GROUP = 8


def inner_kernel(odd_ref, coef_ref, v_ref, s_ref, f_ref, kept_ref, there_ref, back_ref, rows_ref, r_ref, sp_ref, a_ref, b_ref, sum_ref, acc_ref):
    _, count, rows, width = v_ref.shape
    tiles = width // 128
    odd = odd_ref[0]
    rho = ratios(coef_ref)

    there_ref[...] = shuffle(width)
    acc_ref[...] = jnp.zeros_like(acc_ref)
    for ref in (r_ref, a_ref, b_ref):
        ref[rows] = jnp.zeros(ref.shape[1:], jnp.float32)
    spins = s_ref[...].reshape(3 * rows, width) * -(coupling / hopping)
    for t, got in enumerate(moved_exactly(spins, there_ref[...])):
        for y in range(rows):
            for k in range(3):
                row = got[k * rows + y : k * rows + y + 1]
                sp_ref[y, k, :, t * 128 : (t + 1) * 128] = jnp.broadcast_to(row, (LANES, 128))

    def pass_over(dst, src, ratio, own=False):
        sum_ref[...] = src[0]

        @pl.loop(0, rows, step=GROUP)
        def _(start):
            below = [[sum_ref[k, :, t * 128 : (t + 1) * 128] for t in range(tiles)] for k in range(4)]
            for y in [start + i for i in range(GROUP)]:
                here = by_tile((src, (y,)))
                pairs = []
                for k in range(4):
                    right = on_right([x[k] for x in here])
                    pairs.append([right[t] + src[y + 1, k, :, t * 128 : (t + 1) * 128] for t in range(tiles)])
                left = [on_left(x) for x in below]
                for t in range(tiles):
                    x = plus([x[t] for x in pairs], [x[t] for x in left])
                    x = plus(x, on_site(here[t], load(sp_ref, (y,), t), ratio if own else None))
                    if not own:
                        x = plus(x, times(ratio, load(r_ref, (y,), t)))
                    dst(y, t, x)
                below = pairs
            for k in range(4):
                for t in range(tiles):
                    sum_ref[k, :, t * 128 : (t + 1) * 128] = below[k][t]

    def into(ref):
        return lambda y, t, x: save(ref, (y,), t, x)

    def fields(y, t, w):
        save(acc_ref, (y,), t, plus(density(load(r_ref, (y,), t), w), load(acc_ref, (y,), t)))

    @pl.loop(0, count // LANES)
    def _(g):
        states = v_ref[:, pl.ds(pl.multiple_of(g * LANES, LANES), LANES)]
        for t, got in enumerate(moved(states.reshape(4 * LANES * rows, width), there_ref[...])):
            rows_ref[t] = got

        for y in range(rows):
            for comp in range(4):
                for t in range(tiles):
                    at = pl.ds(comp * LANES * rows + y, LANES, stride=rows)
                    r_ref[y, comp, :, t * 128 : (t + 1) * 128] = rows_ref[t, at, :]

        pass_over(into(a_ref), r_ref, rho[3], own=True)
        pass_over(into(b_ref), a_ref, rho[2])
        for side in range(2):
            for i in range(REACH):
                kept_ref[g, side, i] = r_ref[inwards(odd, side, i, rows)]
            kept_ref[g, side, REACH] = a_ref[inwards(odd, side, 0, rows)]
            kept_ref[g, side, REACH + 1] = b_ref[inwards(odd, side, 0, rows)]
        pass_over(into(a_ref), b_ref, rho[1])
        pass_over(fields, a_ref, rho[0])

    for k in range(3):
        for y in range(0, rows, 8):
            for t in range(tiles):
                at = pl.ds(t * 128, 128)
                f_ref[k, y : y + 8, at] = side_by_side([acc_ref[y + i, k, :, at] for i in range(8)])
    back_ref[...] = shuffle(width, back=True)


def inner(odd, coefficients, vectors, spins):
    _, count, rows, width = vectors.shape
    f32 = jnp.float32
    block = block_of(width)
    matrix = jax.ShapeDtypeStruct((block, block), jnp.bfloat16)
    state = pltpu.VMEM((rows + 1, 4, LANES, width), f32)
    vmem = pl.BlockSpec(memory_space=pltpu.VMEM)
    return pl.pallas_call(
        inner_kernel,
        in_specs=[pl.BlockSpec(memory_space=pltpu.SMEM)] * 2 + [vmem] * 2,
        out_specs=[vmem] * 4,
        out_shape=[
            jax.ShapeDtypeStruct((3, rows, width), f32),
            jax.ShapeDtypeStruct((count // LANES, 2, KEPT, 4, LANES, width), f32),
            matrix,
            matrix,
        ],
        scratch_shapes=[
            pltpu.VMEM((width // 128, 4 * LANES * rows, 128), f32),
            state,
            pltpu.VMEM((rows, 3, LANES, width), f32),
            state,
            state,
            pltpu.VMEM((4, LANES, width), f32),
            pltpu.VMEM((rows, 3, LANES, width), f32),
        ],
        compiler_params=pltpu.CompilerParams(vmem_limit_bytes=40 * MIB),
        cost_estimate=pl.CostEstimate(flops=240 * vectors.size, bytes_accessed=8 * MIB, transcendentals=0),
        name="inner",
    )(odd, coefficients, vectors, spins)


SPINS = ("B2", "B1", "A1", "A2", "A3", "B1 to A3")


def prepare(odd, kept_ref, far_ref, near_ref, s_ref, there_ref, sp_ref, halo_ref, g_refs, ratio):
    _, rows, width = s_ref.shape
    parts = kept_ref.shape[0]
    tiles = width // 128
    end = HALO * 4 * parts * LANES
    matrix = there_ref[...]
    lines = []
    for e, ref in enumerate((far_ref, near_ref)):
        for k in range(3):
            at = end + k * HALO
            lines += [ref[at + i : at + i + 1] for i in (1, 0)]
            lines += [s_ref[k, pl.ds(inwards(odd, e, i, rows), 1)] for i in range(3)]
    lines = jnp.concatenate(lines + lines[:2], axis=0) * -(coupling / hopping)
    for t, got in enumerate(moved_exactly(lines, matrix)):
        at = pl.ds(t * 128, 128)
        for e in range(2):
            for k in range(3):
                five = [got[(e * 3 + k) * 5 + i : (e * 3 + k) * 5 + i + 1] for i in range(5)]
                for i, row in enumerate(five + [five[1] + five[2] + five[3] + five[4]]):
                    sp_ref[e, i, k, :, at] = jnp.broadcast_to(row, (LANES, 128))
    for e, ref in enumerate((far_ref, near_ref)):
        for t, got in enumerate(moved(ref[:end].astype(jnp.bfloat16), matrix)):
            got = got.reshape(HALO, 4, parts, LANES, 128)
            for g in range(parts):
                halo_ref[g, e, :, :, :, t * 128 : (t + 1) * 128] = got[:, :, g]

    for e, ref in enumerate(g_refs):
        sums = [None] * tiles
        for g in range(parts):
            own = lambda i: (kept_ref, (g, e, i - 1))
            b1, b2 = (halo_ref, (g, e, 0)), (halo_ref, (g, e, 1))
            a3 = by_tile(own(3))
            sides = [beside([x[k] for x in a3]) for k in range(4)]
            for t in range(tiles):
                w = on_site(a3[t], load(sp_ref, (e, SPINS.index("B1 to A3")), t), ratio)
                w = plus(w, times(4.0, [x[t] for x in sides]), load(*own(4), t))
                here = density(load(*b1, t), w) + density(load(*b2, t), a3[t])
                sums[t] = here if g == 0 else plus(sums[t], here)
        low = (odd if e == 0 else 1 - odd).astype(jnp.float32)
        zero = jnp.zeros((LANES, 128), jnp.float32)
        for t, x in enumerate(sums):
            at = pl.ds(t * 128, 128)
            ref[:8, at] = low * side_by_side([x[i * 3 + k] for k in range(3) for i in range(HALO)] + [zero] * 2)
            ref[8:, at] = (1.0 - low) * side_by_side([x[i * 3 + k] for k in range(3) for i in (1, 0)] + [zero] * 2)


def cross(part, kept_ref, sp_ref, halo_ref, mid_ref, acc_ref, old_ref, rho):
    tiles = halo_ref.shape[-1] // 128

    def one_edge(e):
        spin = lambda name: (sp_ref, (e, SPINS.index(name)))
        own = lambda i: (kept_ref, (part, e, i - 1))
        a_in, b_in = (kept_ref, (part, e, REACH)), (kept_ref, (part, e, REACH + 1))
        b1, b2 = (halo_ref, (part, e, 0)), (halo_ref, (part, e, 1))
        names = ("a_b2", "a_b1", "b_b2", "b_b1", "b_a1", "c_b1", "c_a1", "c_a2", "b1_sides")
        mid = {name: (mid_ref, (e, i)) for i, name in enumerate(names)}
        b1_sides = mid["b1_sides"]

        b1_tiles = by_tile(b1)
        for t, x in enumerate(zip(*lateral(b1_tiles))):
            save(*b1_sides, t, x)

        def make(row, at, others, ratio=None, extra=None):
            if row is b1:
                made = ((t, plus(load(*b1_sides, t), on_site(load(*b1, t), load(*spin(at), t), ratio))) for t in range(tiles))
            else:
                made = flat(by_tile(row), spin(at), ratio)
            for t, x in made:
                for ref, place in others:
                    x = plus(x, load(ref, place, t))
                if extra is not None:
                    x = plus(x, times(extra[0], load(*extra[1], t)))
                yield t, x

        def state(name, *rest, **more):
            for t, x in make(*rest, **more):
                save(*mid[name], t, x)

        def fields(i, r, w):
            for t, x in w:
                x = density(load(*r, t), x)
                if old_ref is not None:
                    x = plus(x, load(old_ref, (e, i), t))
                save(acc_ref, (e, i), t, x)

        state("a_b2", b2, "B2", [b1], ratio=rho[3])
        state("a_b1", b1, "B1", [b2, own(1)], ratio=rho[3])
        state("b_b2", mid["a_b2"], "B2", [mid["a_b1"], b2], extra=(rho[2], b2))
        state("b_b1", mid["a_b1"], "B1", [mid["a_b2"], a_in, b1], extra=(rho[2], b1))
        state("b_a1", b1, "A1", [mid["a_b1"]])
        state("c_b1", mid["b_b1"], "B1", [mid["b_b2"], b_in, mid["b_a1"]], extra=(rho[1], b1))
        state("c_a1", mid["b_a1"], "A1", [mid["b_b1"], b1])
        state("c_a2", b1, "A2", [mid["b_a1"]])
        fields(0, own(1), make(mid["c_a1"], "A1", [mid["c_b1"], mid["c_a2"]]))
        fields(1, own(2), make(mid["c_a2"], "A2", [mid["c_a1"], b1]))
        fields(2, own(3), make(b1, "A3", [mid["c_a2"]]))
        fields(3, own(4), ((t, load(*b1, t)) for t in range(tiles)))

    for e in range(2):
        one_edge(e)


def begin_kernel(odd_ref, coef_ref, kept_ref, far_ref, near_ref, s_ref, there_ref, sp_ref, halo_ref, g_far_ref, g_near_ref):
    rho = ratios(coef_ref)
    prepare(odd_ref[0], kept_ref, far_ref, near_ref, s_ref, there_ref, sp_ref, halo_ref, (g_far_ref, g_near_ref), rho[3])


def begin(odd, coefficients, kept, far, near, spins, there):
    f32 = jnp.float32
    parts, width = kept.shape[0], spins.shape[-1]
    out = [
        (2, len(SPINS), 3, LANES, width),
        (parts, 2, HALO, 4, LANES, width),
        (16, width),
        (16, width),
    ]
    vmem = pl.BlockSpec(memory_space=pltpu.VMEM)
    return pl.pallas_call(
        begin_kernel,
        in_specs=[pl.BlockSpec(memory_space=pltpu.SMEM)] * 2 + [vmem] * 5,
        out_specs=[vmem] * len(out),
        out_shape=[jax.ShapeDtypeStruct(x, f32) for x in out],
        compiler_params=pltpu.CompilerParams(vmem_limit_bytes=32 * MIB),
        cost_estimate=pl.CostEstimate(flops=500 * far.size, bytes_accessed=4 * MIB, transcendentals=0),
        name="begin",
    )(odd, coefficients, kept, far, near, spins, there)


def end_kernel(odd_ref, coef_ref, kept_ref, sp_ref, halo_ref, f_ref, out_ref, mid_ref, acc_ref):
    _, rows, width = f_ref.shape
    parts = kept_ref.shape[0]
    rho = ratios(coef_ref)
    for part in range(parts):
        cross(part, kept_ref, sp_ref, halo_ref, mid_ref, acc_ref, acc_ref if part else None, rho)
    out_ref[...] = f_ref[...]
    half = lax.broadcasted_iota(jnp.int32, (8, 128), 0) < REACH
    for t in range(width // 128):
        at = pl.ds(t * 128, 128)
        for k in range(3):
            low = [acc_ref[odd_ref[0], i, k, :, at] for i in range(REACH)]
            high = [acc_ref[1 - odd_ref[0], i, k, :, at] for i in reversed(range(REACH))]
            edge = side_by_side(low + high)
            out_ref[k, :8, at] += jnp.where(half, edge, 0.0)
            out_ref[k, rows - 8 :, at] += jnp.where(half, 0.0, edge)


def end(odd, coefficients, kept, sp, halo, f):
    f32 = jnp.float32
    vmem = pl.BlockSpec(memory_space=pltpu.VMEM)
    return pl.pallas_call(
        end_kernel,
        in_specs=[pl.BlockSpec(memory_space=pltpu.SMEM)] * 2 + [vmem] * 4,
        out_specs=vmem,
        out_shape=jax.ShapeDtypeStruct(f.shape, f32),
        scratch_shapes=[pltpu.VMEM((2, 9, 4, LANES, f.shape[-1]), f32), pltpu.VMEM((2, REACH, 3, LANES, f.shape[-1]), f32)],
        compiler_params=pltpu.CompilerParams(vmem_limit_bytes=32 * MIB),
        cost_estimate=pl.CostEstimate(flops=300 * kept.size, bytes_accessed=3 * MIB, transcendentals=0),
        name="end",
    )(odd, coefficients, kept, sp, halo, f)


def sine_and_cosine(x):
    quarters = jnp.floor(x * (2.0 / jnp.pi) + 0.5)
    for part in (1.5703125, 4.837512969970703125e-4, 7.54978995489188216e-8):
        x = x - quarters * part
    z = x * x
    sine = ((-1.9515295891e-4 * z + 8.3321608736e-3) * z - 1.6666654611e-1) * z * x + x
    cosine = ((2.443315711809948e-5 * z - 1.388731625493765e-3) * z + 4.166664568298827e-2) * z * z - 0.5 * z + 1.0
    turns = quarters.astype(jnp.int32)
    odd, half = (turns & 1) == 1, (turns & 2) == 2
    sine, cosine = jnp.where(odd, cosine, sine), jnp.where(odd, -sine, cosine)
    return jnp.where(half, -sine, sine), jnp.where(half, -cosine, cosine)


def final_kernel(count_all, coef_ref, s_ref, back_ref, f_ref, other_ref, rotated_ref, fields_ref):
    _, rows, width = s_ref.shape
    total = f_ref[...] + other_ref[...]
    scale = ratios(coef_ref)[4][:1, :1] * (coupling / count_all)
    got = moved_exactly(total.reshape(3 * rows, width), back_ref[...])
    for t, x in enumerate(got):
        at = pl.ds(t * 128, 128)
        field = [x[k * rows : (k + 1) * rows] * scale for k in range(3)]
        spin = [s_ref[k, :, at] for k in range(3)]
        size = jnp.sqrt(field[0] * field[0] + field[1] * field[1] + field[2] * field[2])
        half_angle = (0.5 * time_step) * size
        sine, cosine = sine_and_cosine(half_angle)
        some = half_angle > 0.0
        ratio = jnp.where(some, sine / jnp.where(some, half_angle, 1.0), 1.0)
        along = field[0] * spin[0] + field[1] * spin[1] + field[2] * spin[2]
        keep = 1.0 - 2.0 * sine * sine
        turn = time_step * ratio * cosine
        lift = (0.5 * time_step * time_step) * ratio * ratio * along
        for k in range(3):
            i, j = (k + 1) % 3, (k + 2) % 3
            cross = field[i] * spin[j] - field[j] * spin[i]
            rotated_ref[k, :, at] = keep * spin[k] + turn * cross + lift * field[k]
            fields_ref[k, :, at] = field[k]


def final(coefficients, spins, back, count_all, f, other):
    out = jax.ShapeDtypeStruct(spins.shape, jnp.float32)
    vmem = pl.BlockSpec(memory_space=pltpu.VMEM)
    return pl.pallas_call(
        functools.partial(final_kernel, count_all),
        in_specs=[pl.BlockSpec(memory_space=pltpu.SMEM)] + [vmem] * 4,
        out_specs=[vmem] * 2,
        out_shape=[out, out],
        compiler_params=pltpu.CompilerParams(vmem_limit_bytes=32 * MIB),
        name="final",
    )(coefficients, spins, back, f, other)


def shards(vectors, classical_spins, coefficients):
    across, number = lax.axis_size("vec"), lax.axis_size("lat")
    count_all = vectors.shape[1] * across

    def trade(x, side):
        return lax.ppermute(x, "lat", [(i, (i + (1 if i % 2 != side else -1)) % number) for i in range(number)])

    def swap(x, step):
        steps = across.bit_length() - 1
        bit = lambda i: 1 << (step if i % 2 == 0 else steps - 1 - step)
        pairs = [(i * across + j, i * across + (j ^ bit(i))) for i in range(number) for j in range(across)]
        return lax.ppermute(x, ("lat", "vec"), pairs)

    rows, width = classical_spins.shape[1:]
    odd = jnp.full((1,), lax.rem(lax.axis_index("lat"), 2), jnp.int32)
    far, near, vectors, spins = edges(odd, vectors, classical_spins)
    far, near = trade(far, 0), trade(near, 1)
    f, kept, there, back = inner(odd, coefficients, vectors, spins)
    sp, halo, g_far, g_near = begin(odd, coefficients, kept, far, near, spins, there)
    g_far, g_near = trade(g_far, 0), trade(g_near, 1)
    fields = end(odd, coefficients, kept, sp, halo, f)
    lines = lambda x: x[: 3 * HALO].reshape(3, HALO, width)
    given = g_far + g_near
    fields = fields.at[:, :HALO].add(lines(given)).at[:, rows - HALO :].add(lines(given[8:]))
    steps = across.bit_length() - 1
    if across != 1 << steps or steps == 0:
        return final(coefficients, spins, back, count_all, lax.psum(fields, "vec"), jnp.zeros_like(fields))
    for step in range(steps - 1):
        fields = fields + swap(fields, step)
    return final(coefficients, spins, back, count_all, fields, swap(fields, steps - 1))


def solution(mesh):
    placed = (P(None, "vec", "lat", None), P(None, "lat", None), P())
    return jax.shard_map(
        shards,
        mesh=mesh,
        in_specs=placed,
        out_specs=(P(None, "lat", None), P(None, "lat", None)),
        check_vma=False,
    )
```
